32 devices in a mesh: bucket: 4 (over y, x), seq: 8 (over z, core).
Axes of the slice: x: 2, y: 2, z: 4, core: 2. Of those that a mesh axis runs over, the one named last changes fastest.
Arguments:
- inputs: bfloat16 [8, 8192, 1024], P('bucket', 'seq'), may hold values from -6 to 6
- cotangent: bfloat16 [8, 8192, 1024], P('bucket', 'seq'), may hold values from -6 to 6
- lengths: int32 [8], P('bucket'), may hold values from 4097 to 8192, as said below
- norm_gains: float32 [2, 1024], replicated, may hold values from 0.5 to 1.5
- norm_biases: float32 [2, 1024], replicated, may hold values from -3 to 3
- in_weight: bfloat16 [1024, 3072], replicated, may hold values from -0.1875 to 0.1875
- in_bias: float32 [3072], replicated, may hold values from -2 to 2
- short_conv: float32 [4, 3072], replicated, may hold values from -3 to 3
- long_skip: float32 [1024], replicated, may hold values from -4 to 4
- filter_in: float32 [33, 64], replicated, may hold values from -1 to 1
- filter_mid: float32 [64, 64], replicated, may hold values from -0.75 to 0.75
- filter_vecs: float32 [4, 64], replicated, may hold values from 0.5 to 2
- filter_out: float32 [64, 1024], replicated, may hold values from -0.01171875 to 0.01171875
- decay: float32 [1024], replicated, may hold values from 0 to 1, as said below
- out_weight: bfloat16 [1024, 1024], replicated, may hold values from -0.1875 to 0.1875
- out_bias: float32 [1024], replicated, may hold values from -2 to 2
- up_weight: bfloat16 [1024, 4096], replicated, may hold values from -0.1875 to 0.1875
- up_bias: float32 [4096], replicated, may hold values from -2 to 2
- down_weight: bfloat16 [4096, 1024], replicated, may hold values from -0.09375 to 0.09375
- down_bias: float32 [1024], replicated, may hold values from -2 to 2
Outputs:
- output: bfloat16 [8, 8192, 1024], P('bucket', 'seq')
- input_grad: float32 [8, 8192, 1024], P('bucket', 'seq')
- grad_norm_gains: float32 [2, 1024], P(None, 'seq')
- grad_norm_biases: float32 [2, 1024], P(None, 'seq')
- grad_in_weight: float32 [1024, 3072], P('seq')
- grad_in_bias: float32 [3072], P('seq')
- grad_short_conv: float32 [4, 3072], P(None, 'seq')
- grad_long_skip: float32 [1024], P('seq')
- grad_filter_in: float32 [33, 64], P(None, 'seq')
- grad_filter_mid: float32 [64, 64], P(None, 'seq')
- grad_filter_vecs: float32 [4, 64], P(None, 'seq')
- grad_filter_out: float32 [64, 1024], P(None, 'seq')
- grad_out_weight: float32 [1024, 1024], P('seq')
- grad_out_bias: float32 [1024], P('seq')
- grad_up_weight: float32 [1024, 4096], P('seq')
- grad_up_bias: float32 [4096], P('seq')
- grad_down_weight: float32 [4096, 1024], P('seq')
- grad_down_bias: float32 [1024], P('seq')
The draws below stay inside these ranges and needn't reach their ends.
Inputs may be any that keep to these rules, and one draw needn't show every extreme that they name: `lengths`: every sequence belongs to the bucket of 8192 positions: it is longer than 4096; in each group of 2 sequences one has the full 8192 tokens. `decay`: positive rates.
All inputs are finite; a program needn't handle non-finite values.
Results may differ from the reference program's by a relative error of at most 0.017.
Values may be sent and summed in bfloat16 or wider, within the bound.
No kernel may reach another device: no remote copies, remote signals or barrier semaphores. Data moves between devices by JAX's collectives and lax.ppermute only.
A program may use at most 576 MiB of HBM per device.

```python
import math
import jax
import jax.numpy as jnp
from jax import lax

D = 1024
FF = 4096
FHID = 64
EMB = 33
LEN = 8192
SEQS = 2
N_BUCKET = 4


def draw_lengths(key, part):
    key = jax.random.fold_in(key, 11)
    k_extra, k_pick = jax.random.split(key, 2)
    least = LEN // 2 + 1
    count = N_BUCKET * SEQS
    drawn = jax.random.randint(k_extra, (count,), least, LEN + 1).reshape(N_BUCKET, SEQS)
    pick = jax.random.randint(k_pick, (N_BUCKET,), 0, SEQS)
    slots = jnp.arange(SEQS, dtype=jnp.int32)
    groups = jnp.arange(N_BUCKET, dtype=jnp.int32)
    drawn = jnp.where(slots[None, :] == pick[:, None], LEN, drawn)
    shortest = (groups[:, None] == 0) & (slots[None, :] == (pick[0] + 1) % SEQS)
    drawn = jnp.where(shortest, least, drawn)
    return drawn.reshape(count).astype(jnp.int32)


def draw_decay(key, part):
    key = jax.random.fold_in(key, 23)
    k_rate = jax.random.fold_in(key, 0)
    slow_low = math.log(0.3 / LEN)
    return jnp.exp(jax.random.uniform(k_rate, (D,), jnp.float32, slow_low, math.log(1.0 / 30.0))).astype(jnp.float32)


def draw_filter_in(key, part):
    key = jax.random.fold_in(key, 31)
    return jax.random.uniform(key, (EMB, FHID), jnp.float32, -1.0, 1.0)


def draw_filter_mid(key, part):
    key = jax.random.fold_in(key, 37)
    return jax.random.uniform(key, (FHID, FHID), jnp.float32, -0.75, 0.75)


def draw_filter_vecs(key, part):
    key = jax.random.fold_in(key, 41)
    k_bias, k_freq = jax.random.split(key, 2)
    biases = jax.random.uniform(k_bias, (2, FHID), jnp.float32, 0.5, 2.0)
    freqs = jax.random.uniform(k_freq, (2, FHID), jnp.float32, 1.5, 2.0)
    return jnp.stack([biases[0], freqs[0], biases[1], freqs[1]]).astype(jnp.float32)


def steps_of(stream_key, dims, pieces, smallest, top_value):
    level = 1.0
    for axis_at, parts in pieces:
        heights = jax.random.uniform(jax.random.fold_in(jax.random.fold_in(stream_key, 6), axis_at), (parts,), jnp.float32, smallest / len(pieces), top_value / len(pieces))
        level = level * jnp.repeat(jnp.exp(heights), dims[axis_at] // parts).reshape((-1,) + (1,) * (len(dims) - 1 - axis_at))
    return level


def gaussian(rng, shape, scale, bound, cuts=(), held_as=jnp.bfloat16):
    values = scale * jax.random.normal(rng, shape, jnp.float32)
    if cuts:
        values = values * steps_of(rng, shape, cuts, -0.22, 0.18)
    return jnp.clip(values, -bound, bound).astype(held_as)


def setup_inputs(seed: int = 0) -> dict:
    splits = jax.random.split(jax.random.key(seed), 21)
    inputs = gaussian(splits[0], (N_BUCKET * SEQS, LEN, D), 1.0, 6.0, ((0, 4), (1, 8)))
    cotangent = gaussian(splits[1], (N_BUCKET * SEQS, LEN, D), 1.0, 6.0, ((0, 4), (1, 8)))
    lengths = draw_lengths(jax.random.fold_in(splits[20], 71), 0)
    norm_gains = jnp.clip(1.0 + 0.1 * jax.random.normal(splits[3], (2, D), jnp.float32), 0.5, 1.5)
    norm_biases = gaussian(splits[4], (2, D), 0.5, 3.0, (), jnp.float32)
    in_weight = gaussian(splits[5], (D, 3 * D), D ** -0.5, 0.1875)
    in_bias = gaussian(splits[6], (3 * D,), 0.3, 2.0, (), jnp.float32)
    short_conv = gaussian(splits[7], (4, 3 * D), 0.6, 3.0, (), jnp.float32)
    long_skip = gaussian(splits[8], (D,), 1.0, 4.0, (), jnp.float32)
    filter_in = draw_filter_in(jax.random.fold_in(splits[20], 71), 0)
    filter_mid = draw_filter_mid(jax.random.fold_in(splits[20], 71), 0)
    filter_vecs = draw_filter_vecs(jax.random.fold_in(splits[20], 71), 0)
    filter_out = gaussian(splits[12], (FHID, D), (32 * LEN) ** -0.5, 0.01171875, (), jnp.float32)
    decay = draw_decay(jax.random.fold_in(splits[20], 71), 0)
    out_weight = gaussian(splits[14], (D, D), D ** -0.5, 0.1875)
    out_bias = gaussian(splits[15], (D,), 0.3, 2.0, (), jnp.float32)
    up_weight = gaussian(splits[16], (D, FF), D ** -0.5, 0.1875)
    up_bias = gaussian(splits[17], (FF,), 0.3, 2.0, (), jnp.float32)
    down_weight = gaussian(splits[18], (FF, D), FF ** -0.5, 0.09375)
    down_bias = gaussian(splits[19], (D,), 0.3, 2.0, (), jnp.float32)
    return {"inputs": inputs, "cotangent": cotangent, "lengths": lengths, "norm_gains": norm_gains, "norm_biases": norm_biases, "in_weight": in_weight, "in_bias": in_bias, "short_conv": short_conv, "long_skip": long_skip, "filter_in": filter_in, "filter_mid": filter_mid, "filter_vecs": filter_vecs, "filter_out": filter_out, "decay": decay, "out_weight": out_weight, "out_bias": out_bias, "up_weight": up_weight, "up_bias": up_bias, "down_weight": down_weight, "down_bias": down_bias}


@jax.custom_vjp
def low(v):
    return lax.optimization_barrier(v.astype(jnp.bfloat16)).astype(jnp.float32)

@jax.custom_vjp
def low_back(v):
    return v

def low_keep(v):
    return (low(v), None)

def low_pass(kept, grad):
    return (grad,)

def back_keep(v):
    return (v, None)

def back_low(kept, grad):
    return (low(grad),)
low.defvjp(low_keep, low_pass)
low_back.defvjp(back_keep, back_low)
epsilon = 1e-05

def best_dot(left, right):
    return jnp.dot(left, right, precision=lax.Precision.HIGHEST)

def layer_norm(rows, gain, shift):
    mean = lax.optimization_barrier(jnp.mean(rows, axis=-1, keepdims=True))
    centered = rows - mean
    spread = lax.optimization_barrier(jnp.mean(centered * centered, axis=-1, keepdims=True))
    return centered * lax.rsqrt(spread + epsilon) * gain + shift

def positions_embed(length):
    steps = jnp.arange(length, dtype=jnp.int32)
    bands = jnp.arange((EMB - 1) // 2, dtype=jnp.int32)
    angle = 2.0 * math.pi * (steps[:, None] * bands[None, :] % length).astype(jnp.float32) / length
    first = steps[:, None].astype(jnp.float32) / (length - 1)
    return jnp.concatenate([first, jnp.cos(angle), -jnp.sin(angle)], axis=1)

def filter_taps(filter_in, filter_mid, filter_vecs, filter_out, decay):
    emb = positions_embed(LEN)
    first = jnp.sin(filter_vecs[1] * (best_dot(emb, filter_in) + filter_vecs[0]))
    second = jnp.sin(filter_vecs[3] * (best_dot(first, filter_mid) + filter_vecs[2]))
    steps = jnp.arange(LEN, dtype=jnp.int32).astype(jnp.float32)
    return best_dot(second, filter_out) * jnp.exp(-decay[None, :] * steps[:, None])

def one_sequence(rows, valid, weights, taps):
    gains, shifts, w_in, b_in, short, skip, w_out, b_out, w_up, b_up, w_down, b_down = weights
    width = rows.shape[1]
    normed = low(layer_norm(rows, gains[0], shifts[0]))
    proj = low(low_back(best_dot(normed, w_in) + b_in))
    padded = jnp.concatenate([jnp.zeros((2, proj.shape[1]), jnp.float32), proj], axis=0)
    mixed = short[0] * padded[:-2] + short[1] * padded[1:-1] + short[2] * padded[2:] + short[3]
    gate_out = mixed[:, :width]
    gate_in = mixed[:, width:2 * width]
    value = mixed[:, 2 * width:]
    carried = low(gate_in * value)
    total = 2 * LEN
    spectrum = jnp.fft.rfft(carried, n=total, axis=0) * jnp.fft.rfft(taps, n=total, axis=0)
    conv = jnp.fft.irfft(spectrum, n=total, axis=0)[:LEN]
    long_out = low_back(conv) + skip * carried
    gated = low(gate_out * long_out)
    resid = rows + low_back(best_dot(gated, w_out) + b_out)
    normed2 = low(layer_norm(resid, gains[1], shifts[1]))
    hidden = low_back(best_dot(normed2, w_up) + b_up)
    act = low(jax.nn.gelu(hidden, approximate=False))
    final = resid + low_back(best_dot(act, w_down) + b_down)
    return final * valid[:, None]

def forward(rows, gains, shifts, w_in, b_in, short, skip, f_in, f_mid, f_vecs, f_out, w_out, b_out, w_up, b_up, w_down, b_down, decay, valid):
    taps = filter_taps(f_in, f_mid, f_vecs, f_out, decay)
    weights = (gains, shifts, w_in, b_in, short, skip, w_out, b_out, w_up, b_up, w_down, b_down)
    checked = jax.checkpoint(one_sequence)

    def step(carry, pair):
        return (carry, checked(pair[0], pair[1], weights, taps))
    _, outs = lax.scan(step, jnp.zeros((), jnp.float32), (rows, valid))
    return outs

def reference(inputs, cotangent, lengths, norm_gains, norm_biases, in_weight, in_bias, short_conv, long_skip, filter_in, filter_mid, filter_vecs, filter_out, decay, out_weight, out_bias, up_weight, up_bias, down_weight, down_bias):
    f32 = jnp.float32
    places = jnp.arange(LEN, dtype=jnp.int32)
    valid = (places[None, :] < lengths[:, None]).astype(f32)
    primal = (inputs.astype(f32), norm_gains, norm_biases, in_weight.astype(f32), in_bias, short_conv, long_skip, filter_in, filter_mid, filter_vecs, filter_out, out_weight.astype(f32), out_bias, up_weight.astype(f32), up_bias, down_weight.astype(f32), down_bias)

    def wrapped(*values):
        return forward(*values, decay, valid)
    result, pull = jax.vjp(wrapped, *primal)
    grads = pull(cotangent.astype(f32))
    return (result.astype(jnp.bfloat16), grads[0], grads[1], grads[2], grads[3], grads[4], grads[5], grads[6], grads[7], grads[8], grads[9], grads[10], grads[11], grads[12], grads[13], grads[14], grads[15], grads[16])
```

```python
import functools
import math

import jax
import jax.numpy as jnp
import ml_dtypes
import numpy as np
from jax import lax
from jax.experimental import pallas as pl
from jax.experimental.pallas import tpu as pltpu
from jax.sharding import PartitionSpec as P

EMB = 33
LEN = 8192
HALF = 64
KB = 128
LANES = 128
STEP_K = 16
STEP_F = 16

epsilon = 1e-05
f32 = jnp.float32
bf16 = jnp.bfloat16
MIB = 2**20


def passed_along(block, axis, distance):
    devices = range(lax.axis_size(axis))
    route = [(i - distance, i) for i in devices if i - distance in devices]
    return lax.ppermute(block, axis, route)


def best_dot(left, right):
    return jnp.dot(left, right, precision=lax.Precision.HIGHEST)


def dot(left, right):
    return jnp.dot(left, right, preferred_element_type=f32)


def dot_t(left, right):
    return lax.dot_general(left, right, (((1,), (1,)), ((), ())), preferred_element_type=f32)


def weight_grad(left, right):
    return jnp.einsum("tk,tn->kn", left, right, preferred_element_type=f32)


def positions_embed(length):
    steps = jnp.arange(length, dtype=jnp.int32)
    bands = jnp.arange((EMB - 1) // 2, dtype=jnp.int32)
    angle = 2.0 * math.pi * (steps[:, None] * bands[None, :] % length).astype(f32) / length
    first = steps[:, None].astype(f32) / (length - 1)
    return jnp.concatenate([first, jnp.cos(angle), -jnp.sin(angle)], axis=1)


def filter_taps(filter_in, filter_mid, filter_vecs, columns, rates):
    emb = positions_embed(LEN)
    first = jnp.sin(filter_vecs[1] * (best_dot(emb, filter_in) + filter_vecs[0]))
    second = jnp.sin(filter_vecs[3] * (best_dot(first, filter_mid) + filter_vecs[2]))
    steps = jnp.arange(LEN, dtype=jnp.int32).astype(f32)
    return best_dot(second, columns) * jnp.exp(-rates[None, :] * steps[:, None])


def transform_tables():
    m = np.arange(HALF)
    k = np.arange(KB)
    f = np.arange(HALF)
    turns = ((4 * f[None, :, None] + 1) * (KB * m[None, None, :] + k[:, None, None])) % (4 * LEN)
    phase = 2 * np.pi * turns / (4 * LEN)
    table = np.concatenate([np.cos(phase), -np.sin(phase)], axis=1).astype(np.float32)
    high = table.astype(ml_dtypes.bfloat16)
    low = (table - high.astype(np.float32)).astype(ml_dtypes.bfloat16)
    onward = np.concatenate([high, low, high], axis=2)
    back = np.ascontiguousarray(np.swapaxes(table, 1, 2)).astype(ml_dtypes.bfloat16)
    angle = 2 * np.pi * ((k[:, None] * k[None]) % KB) / KB
    cos, sin = np.cos(angle), np.sin(angle)
    inner = np.block([[cos, sin], [-sin, cos]])
    return (
        jnp.asarray(onward),
        jnp.asarray(back),
        jnp.asarray(inner.astype(ml_dtypes.bfloat16)),
        jnp.asarray(np.ascontiguousarray(inner.T).astype(ml_dtypes.bfloat16)),
    )


def outer_stage(step, exact, src, table, dst):
    for u in range(STEP_K):
        k = step * STEP_K + u
        rows = src[pl.ds(k, HALF, stride=KB), :]
        high = rows.astype(bf16)
        if exact:
            out = dot(table[u, :, : 2 * HALF], jnp.concatenate([high, high], axis=0))
        else:
            low = (rows - high.astype(f32)).astype(bf16)
            out = dot(table[u], jnp.concatenate([high, high, low], axis=0))
        dst[pl.ds(k, HALF, stride=2 * KB), :] = out[:HALF]
        dst[pl.ds(k + KB, HALF, stride=2 * KB), :] = out[HALF:]


def outer_back(step, src, table, dst):
    for u in range(STEP_K):
        k = step * STEP_K + u
        real = src[pl.ds(k, HALF, stride=2 * KB), :]
        imag = src[pl.ds(k + KB, HALF, stride=2 * KB), :]
        rows = jnp.concatenate([real, imag], axis=0).astype(bf16)
        dst[pl.ds(k, HALF, stride=KB), :] = dot(table[u], rows)


OUTER_STEPS = KB // STEP_K
INNER_STEPS = HALF // STEP_F


def conv_kernel(backward, x_ref, h_ref, *refs):
    if backward:
        spec_in, ta, tai, tb, tbi, y_ref, spec_out, xs, mid, ys = refs
    else:
        ta, tai, tb, tbi, y_ref, spec_out, xs, mid, ys = refs
    i = pl.program_id(0)

    @pl.when(i == 0)
    def _():
        xs[...] = x_ref[...].astype(f32)

    @pl.when(i < OUTER_STEPS)
    def _():
        outer_stage(i, True, xs, ta, mid)

    @pl.when((i >= OUTER_STEPS) & (i < OUTER_STEPS + INNER_STEPS))
    def _():
        for u in range(STEP_F // 2):
            row = pl.multiple_of(((i - OUTER_STEPS) * STEP_F + 2 * u) * 2 * KB, 2 * KB)
            left = mid[pl.ds(row, 2 * KB), :].astype(bf16)
            right = mid[pl.ds(row + 2 * KB, 2 * KB), :].astype(bf16)
            spec = dot(tb[...], jnp.concatenate([left, right], axis=1))
            prods = []
            for v in range(2):
                at = 2 * u + v
                re = spec[:KB, v * LANES : (v + 1) * LANES]
                im = spec[KB:, v * LANES : (v + 1) * LANES]
                hr = h_ref[at, :KB]
                hi = h_ref[at, KB:]
                if backward:
                    pr, pi = re * hr + im * hi, im * hr - re * hi
                    sr = spec_in[at, :KB].astype(f32)
                    si = spec_in[at, KB:].astype(f32)
                    spec_out[at, :KB] = (re * sr + im * si).astype(bf16)
                    spec_out[at, KB:] = (im * sr - re * si).astype(bf16)
                else:
                    pr, pi = re * hr - im * hi, re * hi + im * hr
                    spec_out[at, :KB] = re.astype(bf16)
                    spec_out[at, KB:] = im.astype(bf16)
                prods.append(jnp.concatenate([pr, pi], axis=0).astype(bf16))
            out = dot(tbi[...], jnp.concatenate(prods, axis=1))
            mid[pl.ds(row, 2 * KB), :] = out[:, :LANES]
            mid[pl.ds(row + 2 * KB, 2 * KB), :] = out[:, LANES:]

    @pl.when(i >= OUTER_STEPS + INNER_STEPS)
    def _():
        outer_back(i - OUTER_STEPS - INNER_STEPS, mid, tai, ys)

    @pl.when(i == 2 * OUTER_STEPS + INNER_STEPS - 1)
    def _():
        y_ref[...] = (ys[...] * (1.0 / LEN)).astype(bf16)


def whole_spec(shape):
    return pl.BlockSpec(shape, lambda i: (0,) * len(shape))


def once(shape):
    return pl.BlockSpec(shape, lambda i: (0,) * len(shape), pipeline_mode=pl.Buffered(1))


def in_step(shape, first, steps):
    return pl.BlockSpec(shape, lambda i: (jnp.clip(i - first, 0, steps - 1), 0, 0))


def transform_scratch():
    return [
        pltpu.VMEM((LEN, LANES), f32),
        pltpu.VMEM((HALF * 2 * KB, LANES), f32),
        pltpu.VMEM((LEN, LANES), f32),
    ]


def long_conv(rows, taps_spec, tables, data_spec=None):
    backward = data_spec is not None
    onward, back, inner, inner_back = tables
    steps = 2 * OUTER_STEPS + INNER_STEPS
    freq = in_step((STEP_F, 2 * KB, LANES), OUTER_STEPS, INNER_STEPS)
    extra = [data_spec] if backward else []
    return pl.pallas_call(
        functools.partial(conv_kernel, backward),
        grid=(steps,),
        in_specs=[once((LEN, LANES)), freq]
        + [freq] * len(extra)
        + [
            in_step((STEP_K, 2 * HALF, 3 * HALF), 0, OUTER_STEPS),
            in_step((STEP_K, HALF, 2 * HALF), OUTER_STEPS + INNER_STEPS, OUTER_STEPS),
            once((2 * KB, 2 * KB)),
            once((2 * KB, 2 * KB)),
        ],
        out_specs=[whole_spec((LEN, LANES)), freq],
        out_shape=[
            jax.ShapeDtypeStruct((LEN, LANES), bf16),
            jax.ShapeDtypeStruct((HALF, 2 * KB, LANES), bf16),
        ],
        scratch_shapes=transform_scratch(),
        compiler_params=pltpu.CompilerParams(vmem_limit_bytes=48 * MIB),
        cost_estimate=pl.CostEstimate(
            flops=20 * 10**9, bytes_accessed=30 * 10**6, transcendentals=0
        ),
    )(rows, taps_spec, *extra, onward, back, inner, inner_back)


def taps_kernel(x_ref, ta, tb, h_ref, mid):
    i = pl.program_id(0)

    @pl.when(i < OUTER_STEPS)
    def _():
        outer_stage(i, False, x_ref, ta, mid)

    @pl.when(i >= OUTER_STEPS)
    def _():
        for u in range(STEP_F // 2):
            row = pl.multiple_of(((i - OUTER_STEPS) * STEP_F + 2 * u) * 2 * KB, 2 * KB)
            left = mid[pl.ds(row, 2 * KB), :].astype(bf16)
            right = mid[pl.ds(row + 2 * KB, 2 * KB), :].astype(bf16)
            spec = dot(tb[...], jnp.concatenate([left, right], axis=1))
            h_ref[2 * u] = spec[:, :LANES]
            h_ref[2 * u + 1] = spec[:, LANES:]


def taps_transform(taps, tables):
    onward, _, inner, _ = tables
    return pl.pallas_call(
        taps_kernel,
        grid=(OUTER_STEPS + INNER_STEPS,),
        in_specs=[
            once((LEN, LANES)),
            in_step((STEP_K, 2 * HALF, 3 * HALF), 0, OUTER_STEPS),
            once((2 * KB, 2 * KB)),
        ],
        out_specs=in_step((STEP_F, 2 * KB, LANES), OUTER_STEPS, INNER_STEPS),
        out_shape=jax.ShapeDtypeStruct((HALF, 2 * KB, LANES), f32),
        scratch_shapes=transform_scratch()[1:2],
        compiler_params=pltpu.CompilerParams(vmem_limit_bytes=48 * MIB),
        cost_estimate=pl.CostEstimate(
            flops=10 * 10**9, bytes_accessed=18 * 10**6, transcendentals=0
        ),
    )(taps, onward, inner)


def taps_back_kernel(count, *refs):
    specs = refs[:count]
    tai, tbi, y_ref, mid, ys = refs[count:]
    i = pl.program_id(0)

    @pl.when(i < INNER_STEPS)
    def _():
        for u in range(STEP_F // 2):
            row = pl.multiple_of((i * STEP_F + 2 * u) * 2 * KB, 2 * KB)
            prods = []
            for v in range(2):
                total = specs[0][2 * u + v].astype(f32)
                for other in specs[1:]:
                    total = total + other[2 * u + v].astype(f32)
                prods.append(total.astype(bf16))
            out = dot(tbi[...], jnp.concatenate(prods, axis=1))
            mid[pl.ds(row, 2 * KB), :] = out[:, :LANES]
            mid[pl.ds(row + 2 * KB, 2 * KB), :] = out[:, LANES:]

    @pl.when(i >= INNER_STEPS)
    def _():
        outer_back(i - INNER_STEPS, mid, tai, ys)

    @pl.when(i == OUTER_STEPS + INNER_STEPS - 1)
    def _():
        y_ref[...] = ys[...] * (1.0 / LEN)


def taps_back(specs, tables):
    _, back, _, inner_back = tables
    count = len(specs)
    return pl.pallas_call(
        functools.partial(taps_back_kernel, count),
        grid=(OUTER_STEPS + INNER_STEPS,),
        in_specs=[in_step((STEP_F, 2 * KB, LANES), 0, INNER_STEPS)] * count
        + [
            in_step((STEP_K, HALF, 2 * HALF), INNER_STEPS, OUTER_STEPS),
            once((2 * KB, 2 * KB)),
        ],
        out_specs=whole_spec((LEN, LANES)),
        out_shape=jax.ShapeDtypeStruct((LEN, LANES), f32),
        scratch_shapes=transform_scratch()[1:],
        compiler_params=pltpu.CompilerParams(vmem_limit_bytes=48 * MIB),
        cost_estimate=pl.CostEstimate(
            flops=10 * 10**9, bytes_accessed=18 * 10**6, transcendentals=0
        ),
    )(*specs, back, inner_back)


def normalized(rows):
    mean = jnp.mean(rows, axis=-1, keepdims=True)
    centered = rows - mean
    spread = jnp.mean(centered * centered, axis=-1, keepdims=True)
    root = lax.rsqrt(spread + epsilon)
    return centered * root, root


def norm_back(grad, gain, xhat, root):
    g = grad * gain
    mean = jnp.mean(g, axis=-1, keepdims=True)
    along = jnp.mean(g * xhat, axis=-1, keepdims=True)
    return (g - mean - xhat * along) * root


def column_sum(block):
    return jnp.sum(block, axis=0, keepdims=True)


def joined(ref):
    if ref.shape[0] == 1:
        return ref[0]
    return jnp.concatenate([ref[b] for b in range(ref.shape[0])], axis=1)


def spread_out(ref, first, block):
    chans = ref.shape[2]
    width = block.shape[1]
    if chans >= first + width and ref.shape[0] == 1:
        ref[0, :, first : first + width] = block
        return
    for at in range(0, width, chans):
        ref[(first + at) // chans] = block[:, at : at + chans]


def front_kernel(
    x_ref, rim_ref, flag_ref, gain, shift, w_ref, b_ref, short, normed_ref, proj_ref, mixed_ref,
    carried_ref, tail
):
    i = pl.program_id(0)
    tile, dim = x_ref.shape

    @pl.when(i == 0)
    def _():
        rows, _ = normalized(rim_ref[...].astype(f32))
        rows = (rows * gain[...] + shift[...]).astype(bf16)
        edge = (dot(rows, w_ref[...]) + b_ref[...]).astype(bf16).astype(f32)
        tail[...] = edge[8:] * flag_ref[...]

    xhat, _ = normalized(x_ref[...].astype(f32))
    normed = (xhat * gain[...] + shift[...]).astype(bf16)
    normed_ref[...] = normed
    block = 256
    at_row = lax.broadcasted_iota(jnp.int32, (tile, block), 0)
    for first in range(0, dim, block):
        parts = []
        for stream in range(3):
            cols = slice(stream * dim + first, stream * dim + first + block)
            proj = (dot(normed, w_ref[:, cols]) + b_ref[:, cols]).astype(bf16)
            proj_ref[:, cols] = proj
            proj = proj.astype(f32)
            one = jnp.where(at_row == 0, tail[7:8, cols], pltpu.roll(proj, 1, 0))
            two = jnp.where(
                at_row == 0,
                tail[6:7, cols],
                jnp.where(at_row == 1, tail[7:8, cols], pltpu.roll(proj, 2, 0)),
            )
            mixed = (
                short[0:1, cols] * two
                + short[1:2, cols] * one
                + short[2:3, cols] * proj
                + short[3:4, cols]
            )
            mixed_ref[:, cols] = mixed.astype(bf16)
            tail[:, cols] = proj[tile - 8 :]
            parts.append(mixed)
        spread_out(carried_ref, first, (parts[1] * parts[2]).astype(bf16))


def front(rows, rim, flag, gain, shift, weight, bias, short, blocks):
    width, dim = rows.shape
    tile = min(256, width)
    wide = weight.shape[1]
    by_row = lambda cols: pl.BlockSpec((tile, cols), lambda i: (i, 0))
    return pl.pallas_call(
        front_kernel,
        grid=(width // tile,),
        in_specs=[
            by_row(dim),
            once(rim.shape),
            once((1, 1)),
            once((1, dim)),
            once((1, dim)),
            once((dim, wide)),
            once((1, wide)),
            once((4, wide)),
        ],
        out_specs=[
            by_row(dim),
            by_row(wide),
            by_row(wide),
            pl.BlockSpec((blocks, tile, dim // blocks), lambda i: (0, i, 0)),
        ],
        out_shape=[
            jax.ShapeDtypeStruct((width, dim), bf16),
            jax.ShapeDtypeStruct((width, wide), bf16),
            jax.ShapeDtypeStruct((width, wide), bf16),
            jax.ShapeDtypeStruct((blocks, width, dim // blocks), bf16),
        ],
        scratch_shapes=[pltpu.VMEM((8, wide), f32)],
        compiler_params=pltpu.CompilerParams(vmem_limit_bytes=48 * MIB),
        cost_estimate=pl.CostEstimate(
            flops=2 * width * dim * wide, bytes_accessed=24 * 10**6, transcendentals=0
        ),
    )(rows, rim, flag, gain, shift, weight, bias, short)


def gelu_and_slope(hidden):
    size = jnp.abs(hidden)
    bell = jnp.exp(hidden * hidden * -0.5)
    t = pl.reciprocal(1.0 + size * (0.3275911 / math.sqrt(2.0)), approx=False)
    poly = 0.5 * 1.061405429
    for term in (-1.453152027, 1.421413741, -0.284496736, 0.254829592):
        poly = poly * t + 0.5 * term
    rest = poly * t * bell
    below = jnp.where(hidden >= 0, 1.0 - rest, rest)
    return hidden * below, below + hidden * (bell * (1.0 / math.sqrt(2.0 * math.pi)))


def mid_kernel(
    count_ref, conv_ref, carried_ref, gate_ref, x_ref, cot_ref, skip, gain, shift, w_out, b_out,
    w_up, b_up, w_down, b_down, *refs
):
    (
        out_ref, act_ref, gh_ref, normed_ref, gated_ref, gdi_ref, branch_ref, resid_ref, ggo_ref,
        gconv_ref, d_gain, d_shift, d_down_b, d_up_b, d_out_b, d_skip
    ) = refs[-16:]
    i = pl.program_id(0)
    tile, dim = x_ref.shape
    hid = w_up.shape[1]

    @pl.when(i == 0)
    def _():
        for ref in (d_gain, d_shift, d_down_b, d_up_b, d_out_b, d_skip):
            ref[...] = jnp.zeros_like(ref)

    place = i * tile + lax.broadcasted_iota(jnp.int32, (tile, 1), 0)
    mask = (place < count_ref[0]).astype(f32)
    carried = joined(carried_ref).astype(f32)
    gate = gate_ref[...].astype(f32)
    long_out = joined(conv_ref).astype(f32) + skip[...] * carried
    gated = (gate * long_out).astype(bf16)
    gated_ref[...] = gated
    resid = x_ref[...].astype(f32) + dot(gated, w_out[...]) + b_out[...]
    xhat, root = normalized(resid)
    normed = (xhat * gain[...] + shift[...]).astype(bf16)
    normed_ref[...] = normed
    grad_final = cot_ref[...].astype(f32) * mask
    gdi = grad_final.astype(bf16)
    gdi_ref[...] = gdi
    d_down_b[...] += column_sum(grad_final)
    final = resid + b_down[...]
    back = jnp.zeros((tile, dim), f32)
    block = 512
    for first in range(0, hid, block):
        cols = slice(first, first + block)
        hidden = dot(normed, w_up[:, cols]) + b_up[:, cols]
        grad_act = dot_t(gdi, w_down[cols, :])
        act, slope = gelu_and_slope(hidden)
        act = act.astype(bf16)
        grad_hidden = (slope * grad_act).astype(bf16)
        act_ref[:, cols] = act
        gh_ref[:, cols] = grad_hidden
        d_up_b[:, cols] += column_sum(grad_hidden.astype(f32))
        final = final + dot(act, w_down[cols, :])
        back = back + dot_t(grad_hidden, w_up[:, cols])
    out_ref[...] = (final * mask).astype(bf16)
    d_shift[...] += column_sum(back)
    d_gain[...] += column_sum(back * xhat)
    grad_resid = grad_final + norm_back(back, gain[...], xhat, root)
    resid_ref[...] = grad_resid
    branch = grad_resid.astype(bf16)
    branch_ref[...] = branch
    d_out_b[...] += column_sum(branch.astype(f32))
    grad_gated = dot_t(branch, w_out[...])
    ggo_ref[...] = (grad_gated * long_out).astype(bf16)
    grad_long = grad_gated * gate
    d_skip[...] += column_sum(grad_long * carried)
    spread_out(gconv_ref, 0, grad_long.astype(bf16))


def middle(s, seqs, count, conv, carried, mixed, rows, cot, skip, gain, shift, w_out, b_out, w_up,
           b_up, w_down, b_down, shared):
    width, dim = rows.shape
    hid = w_up.shape[1]
    blocks, _, chans = carried.shape
    tile = min(256, width)
    tiles = width // tile
    by_row = lambda cols: pl.BlockSpec((tile, cols), lambda i: (i, 0))
    split = pl.BlockSpec((blocks, tile, chans), lambda i: (0, i, 0))
    stacked = lambda cols: pl.BlockSpec((tile, cols), lambda i: (i + s * tiles, 0))
    tok = seqs * width
    sums = [dim, dim, dim, hid, dim, dim]
    shapes = [
        ((width, dim), bf16),
        ((tok, hid), bf16),
        ((tok, hid), bf16),
        ((tok, dim), bf16),
        ((tok, dim), bf16),
        ((tok, dim), bf16),
        ((tok, dim), bf16),
        ((width, dim), f32),
        ((width, dim), bf16),
        ((blocks, width, chans), bf16),
    ] + [((1, n), f32) for n in sums]
    operands = (count, conv, carried, mixed, rows, cot, skip, gain, shift, w_out, b_out, w_up, b_up,
                w_down, b_down)
    aliases = {len(operands) + n: 1 + n for n in range(len(shared))}
    return pl.pallas_call(
        mid_kernel,
        grid=(tiles,),
        in_specs=[
            pl.BlockSpec(memory_space=pltpu.SMEM),
            split,
            split,
            by_row(dim),
            by_row(dim),
            by_row(dim),
            once((1, dim)),
            once((1, dim)),
            once((1, dim)),
            once((dim, dim)),
            once((1, dim)),
            once((dim, hid)),
            once((1, hid)),
            once((hid, dim)),
            once((1, dim)),
        ] + [pl.BlockSpec(memory_space=pl.ANY)] * len(shared),
        out_specs=[
            by_row(dim),
            stacked(hid),
            stacked(hid),
            stacked(dim),
            stacked(dim),
            stacked(dim),
            stacked(dim),
            by_row(dim),
            by_row(dim),
            split,
        ] + [whole_spec((1, n)) for n in sums],
        out_shape=[jax.ShapeDtypeStruct(shape, kind) for shape, kind in shapes],
        input_output_aliases=aliases,
        compiler_params=pltpu.CompilerParams(vmem_limit_bytes=60 * MIB),
        cost_estimate=pl.CostEstimate(
            flops=4 * width * dim * (dim + 2 * hid), bytes_accessed=60 * 10**6,
            transcendentals=2 * width * hid
        ),
    )(*operands, *shared)


def back_kernel(
    gback_ref, gconv_ref, ggo_ref, gates_ref, proj_ref, x_ref, resid_ref, rim_ref, skip, gain,
    short, w_ref, *refs
):
    gproj_ref, igrad_ref, d_gain, d_shift, d_short, d_bias, head = refs[-7:]
    i = pl.program_id(0)
    tile, dim = x_ref.shape

    @pl.when(i == 0)
    def _():
        head[...] = rim_ref[...]
        for ref in (d_gain, d_shift, d_short, d_bias):
            ref[...] = jnp.zeros_like(ref)

    grad_carried = joined(gback_ref).astype(f32) + skip[...] * joined(gconv_ref).astype(f32)
    block = 256
    at_row = lax.broadcasted_iota(jnp.int32, (tile, block), 0)
    grad_normed = jnp.zeros((tile, dim), f32)
    for stream in range(3):
        for first in range(0, dim, block):
            cols = slice(stream * dim + first, stream * dim + first + block)
            if stream == 0:
                now = ggo_ref[:, first : first + block].astype(f32)
            elif stream == 1:
                now = grad_carried[:, first : first + block] * gates_ref[
                    :, 2 * dim + first : 2 * dim + first + block
                ].astype(f32)
            else:
                now = grad_carried[:, first : first + block] * gates_ref[
                    :, dim + first : dim + first + block
                ].astype(f32)
            one = jnp.where(at_row == tile - 1, head[0:1, cols], pltpu.roll(now, tile - 1, 0))
            two = jnp.where(
                at_row == tile - 1,
                head[1:2, cols],
                jnp.where(at_row == tile - 2, head[0:1, cols], pltpu.roll(now, tile - 2, 0)),
            )
            head[:, cols] = now[:8]
            proj = proj_ref[:, cols].astype(f32)
            d_short[0:1, cols] += column_sum(two * proj)
            d_short[1:2, cols] += column_sum(one * proj)
            d_short[2:3, cols] += column_sum(now * proj)
            d_short[3:4, cols] += column_sum(now)
            grad = short[2:3, cols] * now + short[1:2, cols] * one + short[0:1, cols] * two
            grad = grad.astype(bf16)
            gproj_ref[:, cols] = grad
            d_bias[:, cols] += column_sum(grad.astype(f32))
            grad_normed = grad_normed + dot_t(grad, w_ref[:, cols])
    xhat, root = normalized(x_ref[...].astype(f32))
    d_shift[...] += column_sum(grad_normed)
    d_gain[...] += column_sum(grad_normed * xhat)
    igrad_ref[...] = resid_ref[...] + norm_back(grad_normed, gain[...], xhat, root)


def backmost(s, seqs, gback, gconv, ggo, mixed, proj, rows, resid, rim, skip, gain, short, weight,
             shared):
    width, dim = rows.shape
    wide = weight.shape[1]
    blocks, _, chans = gback.shape
    tile = min(256, width)
    tiles = width // tile
    by_row = lambda cols: pl.BlockSpec((tile, cols), lambda i: (tiles - 1 - i, 0))
    split = pl.BlockSpec((blocks, tile, chans), lambda i: (0, tiles - 1 - i, 0))
    operands = (gback, gconv, ggo, mixed, proj, rows, resid, rim, skip, gain, short, weight)
    aliases = {len(operands) + n: n for n in range(len(shared))}
    return pl.pallas_call(
        back_kernel,
        grid=(tiles,),
        in_specs=[
            split,
            split,
            by_row(dim),
            by_row(wide),
            by_row(wide),
            by_row(dim),
            by_row(dim),
            once((8, wide)),
            once((1, dim)),
            once((1, dim)),
            once((4, wide)),
            once((dim, wide)),
        ] + [pl.BlockSpec(memory_space=pl.ANY)] * len(shared),
        out_specs=[
            pl.BlockSpec((tile, wide), lambda i: (s * tiles + tiles - 1 - i, 0)),
            by_row(dim),
            whole_spec((1, dim)),
            whole_spec((1, dim)),
            whole_spec((4, wide)),
            whole_spec((1, wide)),
        ],
        out_shape=[
            jax.ShapeDtypeStruct((seqs * width, wide), bf16),
            jax.ShapeDtypeStruct((width, dim), f32),
            jax.ShapeDtypeStruct((1, dim), f32),
            jax.ShapeDtypeStruct((1, dim), f32),
            jax.ShapeDtypeStruct((4, wide), f32),
            jax.ShapeDtypeStruct((1, wide), f32),
        ],
        input_output_aliases=aliases,
        scratch_shapes=[pltpu.VMEM((8, wide), f32)],
        compiler_params=pltpu.CompilerParams(vmem_limit_bytes=56 * MIB),
        cost_estimate=pl.CostEstimate(
            flops=2 * width * dim * wide, bytes_accessed=30 * 10**6, transcendentals=0
        ),
    )(*operands, *shared)


def on_device(
    inputs,
    cotangent,
    lengths,
    norm_gains,
    norm_biases,
    in_weight,
    in_bias,
    short_conv,
    long_skip,
    filter_in,
    filter_mid,
    filter_vecs,
    filter_out,
    decay,
    out_weight,
    out_bias,
    up_weight,
    up_bias,
    down_weight,
    down_bias,
):
    seqs, width, dim = inputs.shape
    parts = lax.axis_size("seq")
    index = lax.axis_index("seq")
    chans = dim // parts
    fits = chans % LANES == 0
    blocks = parts if fits else 1
    row = lambda v: v.reshape(1, -1)
    gain1, gain2 = norm_gains[0:1], norm_gains[1:2]
    shift1, shift2 = norm_biases[0:1], norm_biases[1:2]
    skip = row(long_skip)
    tables = transform_tables()

    def to_channels(block):
        if not fits:
            block = jnp.swapaxes(block.reshape(width, parts, chans), 0, 1)
        got = lax.all_to_all(block, "seq", split_axis=0, concat_axis=0, tiled=True)
        got = got.reshape(LEN, chans)
        return got if fits else jnp.pad(got, ((0, 0), (0, LANES - chans)))

    def to_positions(block):
        block = block[:, :chans].reshape(parts, width, chans)
        got = lax.all_to_all(block, "seq", split_axis=0, concat_axis=0, tiled=True)
        return got if fits else jnp.swapaxes(got, 0, 1).reshape(1, width, dim)

    rims = passed_along(inputs[:, width - 2 :, :], "seq", 1)
    rims = jnp.pad(rims, ((0, 0), (14, 0), (0, 0)))
    flag = (index > 0).astype(f32).reshape(1, 1)
    counts = jnp.clip(lengths - index * width, 0, width)

    fronts, data = [], []
    for s in range(seqs):
        fronts.append(
            front(inputs[s], rims[s], flag, gain1, shift1, in_weight, row(in_bias), short_conv,
                  blocks)
        )
        data.append(to_channels(fronts[s][3]))

    start = index * chans
    columns = lax.dynamic_slice_in_dim(filter_out, start, chans, 1)
    rates = lax.dynamic_slice_in_dim(decay, start, chans, 0)

    def make_taps(first_w, mid_w, vecs, cols):
        return filter_taps(first_w, mid_w, vecs, cols, rates)

    taps, taps_pull = jax.vjp(make_taps, filter_in, filter_mid, filter_vecs, columns)
    taps_spec = taps_transform(
        taps if fits else jnp.pad(taps, ((0, 0), (0, LANES - chans))), tables
    )

    specs, convs = [], []
    for s in range(seqs):
        conv, spec = long_conv(data[s], taps_spec, tables)
        specs.append(spec)
        convs.append(to_positions(conv))

    mids, grads = [], []
    shared = ()
    for s in range(seqs):
        got = middle(
            s, seqs, counts[s : s + 1], convs[s], fronts[s][3], fronts[s][2], inputs[s],
            cotangent[s], skip, gain2, shift2, out_weight, row(out_bias), up_weight, row(up_bias),
            down_weight, row(down_bias), shared,
        )
        shared = got[1:7]
        mids.append(got)
        grads.append(to_channels(got[9]))
    act, grad_hidden, normed2, gated, grad_down_in, grad_branch = shared

    corrs, gbacks = [], []
    for s in range(seqs):
        back, corr = long_conv(grads[s], taps_spec, tables, specs[s])
        corrs.append(corr)
        gbacks.append(to_positions(back))

    d_down_weight = weight_grad(act, grad_down_in)
    d_up_weight = weight_grad(normed2, grad_hidden)
    d_out_weight = weight_grad(gated, grad_branch)

    grad_taps = taps_back(corrs, tables)[:, :chans]
    d_fin, d_fmid, d_fvecs, d_cols = taps_pull(grad_taps)

    ends = []
    shared = ()
    for s in range(seqs):
        def first_rows(block):
            return jnp.swapaxes(block[:, :2], 0, 1).reshape(2, dim).astype(f32)

        grad_carried = first_rows(gbacks[s]) + skip * first_rows(mids[s][9])
        edge = fronts[s][2][:2].astype(f32)
        rim = jnp.concatenate(
            [
                mids[s][8][:2].astype(f32),
                grad_carried * edge[:, 2 * dim :],
                grad_carried * edge[:, dim : 2 * dim],
            ],
            axis=1,
        )
        rim = jnp.pad(passed_along(rim, "seq", -1), ((0, 6), (0, 0)))
        got = backmost(
            s, seqs, gbacks[s], mids[s][9], mids[s][8], fronts[s][2], fronts[s][1], inputs[s],
            mids[s][7], rim, skip, gain1, short_conv, in_weight, shared,
        )
        shared = got[:1]
        ends.append(got)
    normed = jnp.concatenate([fronts[s][0] for s in range(seqs)], axis=0)
    d_in_weight = weight_grad(normed, shared[0])

    output = jnp.stack([mids[s][0] for s in range(seqs)])
    input_grad = jnp.stack([ends[s][1] for s in range(seqs)])

    def summed(pieces):
        total = pieces[0]
        for piece in pieces[1:]:
            total = total + piece
        return total

    mid_sum = [summed([mids[s][10 + n] for s in range(seqs)]) for n in range(6)]
    end_sum = [summed([ends[s][2 + n] for s in range(seqs)]) for n in range(4)]
    small = [
        jnp.concatenate([end_sum[0], mid_sum[0]], axis=0),
        jnp.concatenate([end_sum[1], mid_sum[1]], axis=0),
        end_sum[3].reshape(-1),
        end_sum[2],
        mid_sum[5].reshape(-1),
        d_fin,
        d_fmid,
        d_fvecs,
        mid_sum[4].reshape(-1),
        mid_sum[3].reshape(-1),
        mid_sum[2].reshape(-1),
    ]
    flat = jnp.concatenate([piece.reshape(-1) for piece in small])
    flat = lax.psum(flat, ("bucket", "seq"))
    shares = []
    at = 0
    for piece in small:
        whole = flat[at : at + piece.size].reshape(piece.shape)
        at += piece.size
        share = piece.shape[-1] // parts
        shares.append(lax.dynamic_slice_in_dim(whole, index * share, share, piece.ndim - 1))
    d_gains, d_shifts, d_in_bias, d_short, d_skip, d_fin, d_fmid, d_fvecs, d_out_b, d_up_b, d_down_b = shares
    d_fout = lax.psum(d_cols, "bucket")

    def shared_sum(block):
        part = lax.psum_scatter(block.astype(bf16), "seq", scatter_dimension=0, tiled=True)
        return lax.psum(part, "bucket").astype(f32)

    return (
        output,
        input_grad,
        d_gains,
        d_shifts,
        shared_sum(d_in_weight),
        d_in_bias,
        d_short,
        d_skip,
        d_fin,
        d_fmid,
        d_fvecs,
        d_fout,
        shared_sum(d_out_weight),
        d_out_b,
        shared_sum(d_up_weight),
        d_up_b,
        shared_sum(d_down_weight),
        d_down_b,
    )


def solution(mesh):
    whole = P()
    in_specs = (P("bucket", "seq", None),) * 2 + (P("bucket"),) + (whole,) * 17
    rows, cols, flat = P("seq", None), P(None, "seq"), P("seq")
    out_specs = (
        P("bucket", "seq", None),
        P("bucket", "seq", None),
        cols,
        cols,
        rows,
        flat,
        cols,
        flat,
        cols,
        cols,
        cols,
        cols,
        rows,
        flat,
        rows,
        flat,
        rows,
        flat,
    )
    return jax.shard_map(
        on_device, mesh=mesh, in_specs=in_specs, out_specs=out_specs, check_vma=False
    )
```

```python
import functools
import math

import jax
import jax.numpy as jnp
import ml_dtypes
import numpy as np
from jax import lax
from jax.experimental import pallas as pl
from jax.experimental.pallas import tpu as pltpu
from jax.sharding import PartitionSpec as P

EMB = 33
LEN = 8192
HALF = 64
KB = 128
LANES = 128
STEP_K = 32
STEP_F = 8
ROWS_K = KB + 1
ROWS_F = 2 * KB + 1
MID_TILE = 256
MID_BLOCK = 512

epsilon = 1e-05
f32 = jnp.float32
bf16 = jnp.bfloat16
MIB = 2**20


def lasting(micros):
    return pl.CostEstimate(
        flops=int(micros * 1.1e9), bytes_accessed=1000, transcendentals=0
    )


def passed_along(block, axis, distance):
    devices = range(lax.axis_size(axis))
    route = [(i - distance, i) for i in devices if i - distance in devices]
    return lax.ppermute(block, axis, route)


def best_dot(left, right):
    return jnp.dot(left, right, precision=lax.Precision.HIGHEST)


def dot(left, right):
    return jnp.dot(left, right, preferred_element_type=f32)


def dot_t(left, right):
    return lax.dot_general(left, right, (((1,), (1,)), ((), ())), preferred_element_type=f32)


def positions_embed(length):
    steps = jnp.arange(length, dtype=jnp.int32)
    bands = jnp.arange((EMB - 1) // 2, dtype=jnp.int32)
    angle = 2.0 * math.pi * (steps[:, None] * bands[None, :] % length).astype(f32) / length
    first = steps[:, None].astype(f32) / (length - 1)
    return jnp.concatenate([first, jnp.cos(angle), -jnp.sin(angle)], axis=1)


def filter_taps(filter_in, filter_mid, filter_vecs, columns, rates):
    emb = positions_embed(LEN)
    first = jnp.sin(filter_vecs[1] * (best_dot(emb, filter_in) + filter_vecs[0]))
    second = jnp.sin(filter_vecs[3] * (best_dot(first, filter_mid) + filter_vecs[2]))
    steps = jnp.arange(LEN, dtype=jnp.int32).astype(f32)
    return best_dot(second, columns) * jnp.exp(-rates[None, :] * steps[:, None])


def transform_tables():
    m = np.arange(HALF)
    k = np.arange(KB)
    f = np.arange(HALF)
    turns = ((4 * f[None, :, None] + 1) * (KB * m[None, None, :] + k[:, None, None])) % (4 * LEN)
    phase = 2 * np.pi * turns / (4 * LEN)
    table = np.concatenate([np.cos(phase), -np.sin(phase)], axis=1).astype(np.float32)
    high = table.astype(ml_dtypes.bfloat16)
    low = (table - high.astype(np.float32)).astype(ml_dtypes.bfloat16)
    onward = np.concatenate([high, low], axis=2)
    back = np.ascontiguousarray(np.swapaxes(table, 1, 2)).astype(ml_dtypes.bfloat16)
    angle = 2 * np.pi * ((k[:, None] * k[None]) % KB) / KB
    cos, sin = np.cos(angle), np.sin(angle)
    inner = np.block([[cos, sin], [-sin, cos]])
    return (
        jnp.asarray(onward),
        jnp.asarray(back),
        jnp.asarray(inner.astype(ml_dtypes.bfloat16)),
        jnp.asarray(np.ascontiguousarray(inner.T).astype(ml_dtypes.bfloat16)),
    )


def looped(count, unroll, body):
    def step(i, carry):
        for u in range(unroll):
            body(i * unroll + u)
        return carry

    lax.fori_loop(0, count // unroll, step, 0)


def fetch(src, dst, sems, first, pieces):
    rows = dst.shape[0] // pieces
    copies = []
    for n in range(pieces):
        part = pl.ds(n * rows, rows)
        copy = pltpu.make_async_copy(src.at[part], dst.at[part], sems.at[first + n])
        copy.start()
        copies.append(copy)
    return copies


def outer_stage(first, count, exact, src, table, dst):
    def body(n):
        k = first + n
        rows = src[pl.ds(k, HALF, stride=ROWS_K), :]
        high = rows.astype(bf16)
        out = dot(table[k], jnp.concatenate([high, high], axis=0))
        if not exact:
            low = (rows - high.astype(f32)).astype(bf16)
            out = out + dot(table[k, :, :HALF], low)
        dst[pl.ds(k, HALF, stride=ROWS_F), :] = out[:HALF]
        dst[pl.ds(k + KB, HALF, stride=ROWS_F), :] = out[HALF:]

    looped(count, STEP_K, body)


def outer_back(first, count, src, table, dst):
    def body(n):
        k = first + n
        real = src[pl.ds(k, HALF, stride=ROWS_F), :]
        imag = src[pl.ds(k + KB, HALF, stride=ROWS_F), :]
        rows = jnp.concatenate([real, imag], axis=0).astype(bf16)
        dst[pl.ds(k, HALF, stride=ROWS_K), :] = dot(table[k], rows)

    looped(count, STEP_K, body)


def spaced(src, dst, first, count):
    for m in range(first, first + count):
        dst[m * ROWS_K : m * ROWS_K + KB] = src[m * KB : (m + 1) * KB].astype(f32)


def packed(src, dst):
    for m in range(HALF):
        rows = src[m * ROWS_K : m * ROWS_K + KB] * (1.0 / LEN)
        dst[m * KB : (m + 1) * KB] = rows.astype(dst.dtype)


def row_pair(at):
    row = at * (2 * ROWS_F)
    return pl.ds(row, 2 * KB), pl.ds(row + ROWS_F, 2 * KB)


PIECES = 4


def conv_kernel(backward, x_ref, h_ref, *refs):
    if backward:
        spec_in, *refs = refs
    ta_ref, tai_ref, tb, tbi = refs[:4]
    y_ref, spec_ref, token, x, h, spec, ta, tai, xs, mid, sems = refs[-11:]
    token[...] = jnp.zeros_like(token)
    x_in = fetch(x_ref, x, sems, 0, 2)
    ta_in = fetch(ta_ref, ta, sems, 2, PIECES)
    h_in = fetch(h_ref, h, sems, 2 + PIECES, PIECES)
    s_in = fetch(spec_in, spec, sems, 2 + 2 * PIECES, PIECES) if backward else ()
    tai_in = fetch(tai_ref, tai, sems, 2 + 3 * PIECES, 1)
    half = HALF // 2
    for n in range(2):
        x_in[n].wait()
        spaced(x, xs, n * half, half)
    for n in range(PIECES):
        ta_in[n].wait()
        outer_stage(n * KB // PIECES, KB // PIECES, True, xs, ta, mid)

    def inner(first):
        def body(n):
            at = first + n
            left, right = row_pair(at)
            both = jnp.concatenate([mid[left, :].astype(bf16), mid[right, :].astype(bf16)], axis=1)
            freq = dot(tb[...], both)
            prods = []
            for v in range(2):
                f = 2 * at + v
                re = freq[:KB, v * LANES : (v + 1) * LANES]
                im = freq[KB:, v * LANES : (v + 1) * LANES]
                hr = h[f, :KB].astype(f32)
                hi = h[f, KB:].astype(f32)
                if backward:
                    pr, pi = re * hr + im * hi, im * hr - re * hi
                    sr = spec[f, :KB].astype(f32)
                    si = spec[f, KB:].astype(f32)
                    spec[f, :KB] = (re * sr + im * si).astype(bf16)
                    spec[f, KB:] = (im * sr - re * si).astype(bf16)
                else:
                    pr, pi = re * hr - im * hi, re * hi + im * hr
                    spec[f, :KB] = re.astype(bf16)
                    spec[f, KB:] = im.astype(bf16)
                prods.append(jnp.concatenate([pr, pi], axis=0).astype(bf16))
            out = dot(tbi[...], jnp.concatenate(prods, axis=1))
            mid[left, :] = out[:, :LANES]
            mid[right, :] = out[:, LANES:]

        return body

    leaving = []
    rows = HALF // PIECES
    for n in range(PIECES):
        h_in[n].wait()
        if backward:
            s_in[n].wait()
        looped(rows // 2, STEP_F, inner(n * rows // 2))
        part = pl.ds(n * rows, rows)
        copy = pltpu.make_async_copy(spec.at[part], spec_ref.at[part], sems.at[3 + 3 * PIECES + n])
        copy.start()
        leaving.append(copy)
    tai_in[0].wait()
    outer_back(0, KB, mid, tai, xs)
    packed(xs, y_ref)
    for copy in leaving:
        copy.wait()


def whole_spec(shape):
    return pl.BlockSpec(shape, lambda i: (0,) * len(shape))


def once(shape):
    return pl.BlockSpec(shape, lambda i: (0,) * len(shape), pipeline_mode=pl.Buffered(1))


TOKEN = jax.ShapeDtypeStruct((8, LANES), f32)
ANYWHERE = pl.BlockSpec(memory_space=pl.ANY)
IN_VMEM = pl.BlockSpec(memory_space=pltpu.VMEM)
SPECTRUM = (HALF, 2 * KB, LANES)


def long_conv(rows, taps_spec, tables, data_spec=None, after=()):
    backward = data_spec is not None
    onward, back, inner, inner_back = tables
    extra = [data_spec] if backward else []
    return pl.pallas_call(
        functools.partial(conv_kernel, backward),
        in_specs=[ANYWHERE] * (4 + len(extra)) + [IN_VMEM] * 2 + [ANYWHERE] * len(after),
        out_specs=[IN_VMEM, ANYWHERE, IN_VMEM],
        out_shape=[
            jax.ShapeDtypeStruct((LEN, LANES), bf16),
            jax.ShapeDtypeStruct(SPECTRUM, bf16),
            TOKEN,
        ],
        scratch_shapes=[
            pltpu.VMEM((LEN, LANES), bf16),
            pltpu.VMEM(SPECTRUM, bf16),
            pltpu.VMEM(SPECTRUM, bf16),
            pltpu.VMEM(onward.shape, bf16),
            pltpu.VMEM(back.shape, bf16),
            pltpu.VMEM((HALF * ROWS_K, LANES), f32),
            pltpu.VMEM((HALF * ROWS_F, LANES), f32),
            pltpu.SemaphoreType.DMA((3 + 4 * PIECES,)),
        ],
        compiler_params=pltpu.CompilerParams(vmem_limit_bytes=60 * MIB),
        cost_estimate=lasting(14),
    )(rows, taps_spec, *extra, onward, back, inner, inner_back, *after)


def taps_kernel(x_ref, ta_ref, tb, *refs):
    h_ref, x, ta, xs, mid, h, sems = refs[-7:]
    x_in = fetch(x_ref, x, sems, 0, 2)
    ta_in = fetch(ta_ref, ta, sems, 2, PIECES)
    half = HALF // 2
    for n in range(2):
        x_in[n].wait()
        spaced(x, xs, n * half, half)
    for n in range(PIECES):
        ta_in[n].wait()
        outer_stage(n * KB // PIECES, KB // PIECES, False, xs, ta, mid)

    def body(at):
        left, right = row_pair(at)
        both = jnp.concatenate([mid[left, :].astype(bf16), mid[right, :].astype(bf16)], axis=1)
        freq = dot(tb[...], both)
        h[2 * at] = freq[:, :LANES].astype(bf16)
        h[2 * at + 1] = freq[:, LANES:].astype(bf16)

    leaving = []
    rows = HALF // PIECES
    for n in range(PIECES):
        looped(rows // 2, STEP_F, lambda at, n=n: body(n * rows // 2 + at))
        part = pl.ds(n * rows, rows)
        copy = pltpu.make_async_copy(h.at[part], h_ref.at[part], sems.at[2 + PIECES + n])
        copy.start()
        leaving.append(copy)
    for copy in leaving:
        copy.wait()


def taps_transform(taps, tables, after):
    onward, _, inner, _ = tables
    return pl.pallas_call(
        taps_kernel,
        in_specs=[ANYWHERE, ANYWHERE, IN_VMEM] + [ANYWHERE] * len(after),
        out_specs=ANYWHERE,
        out_shape=jax.ShapeDtypeStruct(SPECTRUM, bf16),
        scratch_shapes=[
            pltpu.VMEM((LEN, LANES), f32),
            pltpu.VMEM(onward.shape, bf16),
            pltpu.VMEM((HALF * ROWS_K, LANES), f32),
            pltpu.VMEM((HALF * ROWS_F, LANES), f32),
            pltpu.VMEM(SPECTRUM, bf16),
            pltpu.SemaphoreType.DMA((2 + 2 * PIECES,)),
        ],
        compiler_params=pltpu.CompilerParams(vmem_limit_bytes=60 * MIB),
        cost_estimate=lasting(15),
    )(taps, onward, inner, *after)


def taps_back_kernel(count, *refs):
    specs = refs[:count]
    tai_ref, tbi = refs[count : count + 2]
    y_ref, token, tai, mid, ys, held, sems = refs[-7:]
    token[...] = jnp.zeros_like(token)
    tai_in = fetch(tai_ref, tai, sems, 0, 1)
    arrivals = [
        fetch(specs[c], held.at[c], sems, 1 + c * PIECES, PIECES) for c in range(count)
    ]

    def body(at):
        left, right = row_pair(at)
        prods = []
        for v in range(2):
            total = held[0, 2 * at + v].astype(f32)
            for c in range(1, count):
                total = total + held[c, 2 * at + v].astype(f32)
            prods.append(total.astype(bf16))
        out = dot(tbi[...], jnp.concatenate(prods, axis=1))
        mid[left, :] = out[:, :LANES]
        mid[right, :] = out[:, LANES:]

    rows = HALF // PIECES
    for n in range(PIECES):
        for c in range(count):
            arrivals[c][n].wait()
        looped(rows // 2, STEP_F, lambda at, n=n: body(n * rows // 2 + at))
    tai_in[0].wait()
    outer_back(0, KB, mid, tai, ys)
    packed(ys, y_ref)


def taps_back(specs, tables, after):
    _, back, _, inner_back = tables
    count = len(specs)
    return pl.pallas_call(
        functools.partial(taps_back_kernel, count),
        in_specs=[ANYWHERE] * (count + 1) + [IN_VMEM] + [ANYWHERE] * len(after),
        out_specs=[IN_VMEM, IN_VMEM],
        out_shape=[jax.ShapeDtypeStruct((LEN, LANES), f32), TOKEN],
        scratch_shapes=[
            pltpu.VMEM(back.shape, bf16),
            pltpu.VMEM((HALF * ROWS_F, LANES), f32),
            pltpu.VMEM((HALF * ROWS_K, LANES), f32),
            pltpu.VMEM((count,) + SPECTRUM, bf16),
            pltpu.SemaphoreType.DMA((1 + count * PIECES,)),
        ],
        compiler_params=pltpu.CompilerParams(vmem_limit_bytes=60 * MIB),
        cost_estimate=lasting(15),
    )(*specs, back, inner_back, *after)


def normalized(rows):
    mean = jnp.mean(rows, axis=-1, keepdims=True)
    centered = rows - mean
    spread = jnp.mean(centered * centered, axis=-1, keepdims=True)
    root = lax.rsqrt(spread + epsilon)
    return centered * root, root


def norm_back(grad, gain, xhat, root):
    g = grad * gain
    mean = jnp.mean(g, axis=-1, keepdims=True)
    along = jnp.mean(g * xhat, axis=-1, keepdims=True)
    return (g - mean - xhat * along) * root


def column_sum(block):
    return jnp.sum(block, axis=0, keepdims=True)


def joined(ref):
    if ref.shape[0] == 1:
        return ref[0]
    return jnp.concatenate([ref[b] for b in range(ref.shape[0])], axis=1)


def spread_out(ref, first, block):
    chans = ref.shape[2]
    width = block.shape[1]
    if chans >= first + width and ref.shape[0] == 1:
        ref[0, :, first : first + width] = block
        return
    for at in range(0, width, chans):
        ref[(first + at) // chans] = block[:, at : at + chans]


def front_kernel(
    x_ref, rim_ref, flag_ref, gain, shift, w_ref, b_ref, short, *refs
):
    normed_ref, proj_ref, mixed_ref, carried_ref, token, tail = refs[-6:]
    i = pl.program_id(0)
    tile, dim = x_ref.shape
    token[...] = jnp.zeros_like(token)

    @pl.when(i == 0)
    def _():
        rows, _ = normalized(rim_ref[...].astype(f32))
        rows = (rows * gain[...] + shift[...]).astype(bf16)
        edge = (dot(rows, w_ref[...]) + b_ref[...]).astype(bf16).astype(f32)
        tail[...] = edge[8:] * flag_ref[...]

    xhat, _ = normalized(x_ref[...].astype(f32))
    normed = (xhat * gain[...] + shift[...]).astype(bf16)
    normed_ref[...] = normed
    block = 256
    at_row = lax.broadcasted_iota(jnp.int32, (tile, block), 0)
    for first in range(0, dim, block):
        parts = []
        for stream in range(3):
            cols = slice(stream * dim + first, stream * dim + first + block)
            proj = (dot(normed, w_ref[:, cols]) + b_ref[:, cols]).astype(bf16)
            proj_ref[:, cols] = proj
            proj = proj.astype(f32)
            one = jnp.where(at_row == 0, tail[7:8, cols], pltpu.roll(proj, 1, 0))
            two = jnp.where(
                at_row == 0,
                tail[6:7, cols],
                jnp.where(at_row == 1, tail[7:8, cols], pltpu.roll(proj, 2, 0)),
            )
            mixed = (
                short[0:1, cols] * two
                + short[1:2, cols] * one
                + short[2:3, cols] * proj
                + short[3:4, cols]
            )
            mixed_ref[:, cols] = mixed.astype(bf16)
            tail[:, cols] = proj[tile - 8 :]
            parts.append(mixed)
        spread_out(carried_ref, first, (parts[1] * parts[2]).astype(bf16))


def front(s, inputs, rims, flag, gain, shift, weight, bias, short, blocks, shared):
    seqs, width, dim = inputs.shape
    tile = min(256, width)
    tiles = width // tile
    wide = weight.shape[1]
    tok = seqs * width
    stacked = lambda cols: pl.BlockSpec((tile, cols), lambda i: (s * tiles + i, 0))
    operands = (inputs, rims, flag, gain, shift, weight, bias, short)
    return pl.pallas_call(
        front_kernel,
        grid=(tiles,),
        in_specs=[
            pl.BlockSpec((None, tile, dim), lambda i: (s, i, 0)),
            pl.BlockSpec((None,) + rims.shape[1:], lambda i: (s, 0, 0)),
            once((1, 1)),
            once((1, dim)),
            once((1, dim)),
            once((dim, wide)),
            once((1, wide)),
            once((4, wide)),
        ]
        + [ANYWHERE] * len(shared),
        out_specs=[
            stacked(dim),
            stacked(wide),
            stacked(wide),
            pl.BlockSpec((blocks, tile, dim // blocks), lambda i: (0, i, 0)),
            whole_spec(TOKEN.shape),
        ],
        out_shape=[
            jax.ShapeDtypeStruct((tok, dim), bf16),
            jax.ShapeDtypeStruct((tok, wide), bf16),
            jax.ShapeDtypeStruct((tok, wide), bf16),
            jax.ShapeDtypeStruct((blocks, width, dim // blocks), bf16),
            TOKEN,
        ],
        input_output_aliases={len(operands) + n: n for n in range(len(shared))},
        scratch_shapes=[pltpu.VMEM((8, wide), f32)],
        compiler_params=pltpu.CompilerParams(vmem_limit_bytes=60 * MIB),
        cost_estimate=lasting(20),
    )(*operands, *shared)


def gelu_and_slope(hidden):
    size = jnp.abs(hidden)
    bell = jnp.exp(hidden * hidden * -0.5)
    t = pl.reciprocal(1.0 + size * (0.3275911 / math.sqrt(2.0)), approx=False)
    poly = 0.5 * 1.061405429
    for term in (-1.453152027, 1.421413741, -0.284496736, 0.254829592):
        poly = poly * t + 0.5 * term
    rest = poly * t * bell
    below = jnp.where(hidden >= 0, 1.0 - rest, rest)
    return hidden * below, below + hidden * (bell * (1.0 / math.sqrt(2.0 * math.pi)))


def mid_kernel(
    count_ref, conv_ref, carried_ref, gate_ref, x_ref, cot_ref, skip, gain, shift, w_out, b_out,
    w_up, b_up, w_down, b_down, *refs
):
    (
        out_ref, act_ref, gh_ref, normed_ref, gated_ref, gdi_ref, branch_ref, resid_ref, ggo_ref,
        gconv_ref, d_gain, d_shift, d_down_b, d_up_b, d_out_b, d_skip
    ) = refs[-16:]
    i = pl.program_id(0)
    tile, dim = x_ref.shape
    hid = w_up.shape[1]

    @pl.when(i == 0)
    def _():
        for ref in (d_gain, d_shift, d_down_b, d_up_b, d_out_b, d_skip):
            ref[...] = jnp.zeros_like(ref)

    place = i * tile + lax.broadcasted_iota(jnp.int32, (tile, 1), 0)
    mask = (place < count_ref[0]).astype(f32)
    carried = joined(carried_ref).astype(f32)
    gate = gate_ref[...].astype(f32)
    long_out = joined(conv_ref).astype(f32) + skip[...] * carried
    gated = (gate * long_out).astype(bf16)
    gated_ref[...] = gated
    resid = x_ref[...].astype(f32) + dot(gated, w_out[...]) + b_out[...]
    xhat, root = normalized(resid)
    normed = (xhat * gain[...] + shift[...]).astype(bf16)
    normed_ref[...] = normed
    grad_final = cot_ref[...].astype(f32) * mask
    gdi = grad_final.astype(bf16)
    gdi_ref[...] = gdi
    d_down_b[...] += column_sum(grad_final)
    final = resid + b_down[...]
    back = jnp.zeros((tile, dim), f32)
    block = MID_BLOCK
    for first in range(0, hid, block):
        cols = slice(first, first + block)
        hidden = dot(normed, w_up[:, cols]) + b_up[:, cols]
        grad_act = dot_t(gdi, w_down[cols, :])
        act, slope = gelu_and_slope(hidden)
        act = act.astype(bf16)
        grad_hidden = (slope * grad_act).astype(bf16)
        act_ref[:, cols] = act
        gh_ref[:, cols] = grad_hidden
        d_up_b[:, cols] += column_sum(grad_hidden.astype(f32))
        final = final + dot(act, w_down[cols, :])
        back = back + dot_t(grad_hidden, w_up[:, cols])
    out_ref[...] = (final * mask).astype(bf16)
    d_shift[...] += column_sum(back)
    d_gain[...] += column_sum(back * xhat)
    grad_resid = grad_final + norm_back(back, gain[...], xhat, root)
    resid_ref[...] = grad_resid
    branch = grad_resid.astype(bf16)
    branch_ref[...] = branch
    d_out_b[...] += column_sum(branch.astype(f32))
    grad_gated = dot_t(branch, w_out[...])
    ggo_ref[...] = (grad_gated * long_out).astype(bf16)
    grad_long = grad_gated * gate
    d_skip[...] += column_sum(grad_long * carried)
    spread_out(gconv_ref, 0, grad_long.astype(bf16))


def middle(s, count, conv, carried, mixed, inputs, cot, skip, gain, shift, w_out, b_out, w_up,
           b_up, w_down, b_down, shared, after):
    seqs, width, dim = inputs.shape
    hid = w_up.shape[1]
    blocks, _, chans = carried.shape
    tile = min(MID_TILE, width)
    tiles = width // tile
    split = pl.BlockSpec((blocks, tile, chans), lambda i: (0, i, 0))
    stacked = lambda cols: pl.BlockSpec((tile, cols), lambda i: (i + s * tiles, 0))
    layer = pl.BlockSpec((None, tile, dim), lambda i: (s, i, 0))
    tok = seqs * width
    sums = [dim, dim, dim, hid, dim, dim]
    shapes = [
        ((seqs, width, dim), bf16),
        ((tok, hid), bf16),
        ((tok, hid), bf16),
        ((tok, dim), bf16),
        ((tok, dim), bf16),
        ((tok, dim), bf16),
        ((tok, dim), bf16),
        ((tok, dim), f32),
        ((tok, dim), bf16),
        ((blocks, width, chans), bf16),
    ] + [((1, n), f32) for n in sums]
    operands = (count, conv, carried, mixed, inputs, cot, skip, gain, shift, w_out, b_out, w_up,
                b_up, w_down, b_down)
    aliases = {len(operands) + n: n for n in range(len(shared))}
    return pl.pallas_call(
        mid_kernel,
        grid=(tiles,),
        in_specs=[
            pl.BlockSpec(memory_space=pltpu.SMEM),
            split,
            split,
            stacked(dim),
            layer,
            layer,
            once((1, dim)),
            once((1, dim)),
            once((1, dim)),
            once((dim, dim)),
            once((1, dim)),
            once((dim, hid)),
            once((1, hid)),
            once((hid, dim)),
            once((1, dim)),
        ]
        + [ANYWHERE] * (len(shared) + len(after)),
        out_specs=[
            layer,
            stacked(hid),
            stacked(hid),
            stacked(dim),
            stacked(dim),
            stacked(dim),
            stacked(dim),
            stacked(dim),
            stacked(dim),
            split,
        ]
        + [whole_spec((1, n)) for n in sums],
        out_shape=[jax.ShapeDtypeStruct(shape, kind) for shape, kind in shapes],
        input_output_aliases=aliases,
        compiler_params=pltpu.CompilerParams(vmem_limit_bytes=60 * MIB),
        cost_estimate=lasting(66),
    )(*operands, *shared, *after)


def grad_rows(now, proj, cols, head, short, out, d_short, d_bias):
    tile, block = now.shape
    at_row = lax.broadcasted_iota(jnp.int32, (tile, block), 0)
    one = jnp.where(at_row == tile - 1, head[0:1, cols], pltpu.roll(now, tile - 1, 0))
    two = jnp.where(
        at_row == tile - 1,
        head[1:2, cols],
        jnp.where(at_row == tile - 2, head[0:1, cols], pltpu.roll(now, tile - 2, 0)),
    )
    head[:, cols] = now[:8]
    proj = proj.astype(f32)
    d_short[0:1, cols] += column_sum(two * proj)
    d_short[1:2, cols] += column_sum(one * proj)
    d_short[2:3, cols] += column_sum(now * proj)
    d_short[3:4, cols] += column_sum(now)
    grad = short[2:3, cols] * now + short[1:2, cols] * one + short[0:1, cols] * two
    grad = grad.astype(bf16)
    out[:, cols] = grad
    d_bias[:, cols] += column_sum(grad.astype(f32))


def gate_kernel(tiles, ggo_ref, proj_ref, rim_ref, short, *refs):
    out, d_short, d_bias, token, head = refs[-5:]
    i = pl.program_id(0)
    dim = ggo_ref.shape[1]
    token[...] = jnp.zeros_like(token)

    @pl.when(i == 0)
    def _():
        d_short[...] = jnp.zeros_like(d_short)
        d_bias[...] = jnp.zeros_like(d_bias)

    @pl.when(i % tiles == 0)
    def _():
        head[...] = rim_ref[...]

    block = 256
    for first in range(0, dim, block):
        cols = slice(first, first + block)
        grad_rows(ggo_ref[:, cols].astype(f32), proj_ref[:, cols], cols, head, short, out, d_short,
                  d_bias)


def gate_grads(seqs, ggo, proj, rims, short, after):
    tok, dim = ggo.shape
    width = tok // seqs
    tile = min(256, width)
    tiles = width // tile
    by_row = pl.BlockSpec(
        (tile, dim), lambda i: ((i // tiles) * tiles + tiles - 1 - i % tiles, 0)
    )
    return pl.pallas_call(
        functools.partial(gate_kernel, tiles),
        grid=(seqs * tiles,),
        in_specs=[
            by_row,
            by_row,
            pl.BlockSpec((None, 8, dim), lambda i: (i // tiles, 0, 0)),
            once((4, dim)),
        ]
        + [ANYWHERE] * len(after),
        out_specs=[by_row, whole_spec((4, dim)), whole_spec((1, dim)), whole_spec(TOKEN.shape)],
        out_shape=[
            jax.ShapeDtypeStruct((tok, dim), bf16),
            jax.ShapeDtypeStruct((4, dim), f32),
            jax.ShapeDtypeStruct((1, dim), f32),
            TOKEN,
        ],
        scratch_shapes=[pltpu.VMEM((8, dim), f32)],
        compiler_params=pltpu.CompilerParams(vmem_limit_bytes=60 * MIB),
        cost_estimate=lasting(7),
    )(ggo, proj, rims, short, *after)


def pair_kernel(gback_ref, gconv_ref, gates_ref, proj_ref, rim_ref, skip, short, *refs):
    out, d_short, d_bias, token, head = refs[-5:]
    i = pl.program_id(0)
    wide = rim_ref.shape[1]
    dim = wide // 2
    token[...] = jnp.zeros_like(token)

    @pl.when(i == 0)
    def _():
        head[...] = rim_ref[...]
        d_short[...] = jnp.zeros_like(d_short)
        d_bias[...] = jnp.zeros_like(d_bias)

    grad_carried = joined(gback_ref).astype(f32) + skip[...] * joined(gconv_ref).astype(f32)
    block = 256
    for first in range(0, dim, block):
        grad = grad_carried[:, first : first + block]
        for stream in range(2):
            cols = slice(stream * dim + first, stream * dim + first + block)
            other = slice(dim + (1 - stream) * dim + first, dim + (1 - stream) * dim + first + block)
            past = slice(dim + cols.start, dim + cols.stop)
            now = grad * gates_ref[:, other].astype(f32)
            grad_rows(now, proj_ref[:, past], cols, head, short, out, d_short, d_bias)


def pair_grads(s, seqs, gback, gconv, mixed, proj, rim, skip, short, shared, after):
    blocks, width, chans = gback.shape
    wide3 = mixed.shape[1]
    dim = blocks * chans
    wide = 2 * dim
    tile = min(256, width)
    tiles = width // tile
    back_row = lambda cols: pl.BlockSpec((tile, cols), lambda i: (s * tiles + tiles - 1 - i, 0))
    split = pl.BlockSpec((blocks, tile, chans), lambda i: (0, tiles - 1 - i, 0))
    operands = (gback, gconv, mixed, proj, rim, skip, short)
    return pl.pallas_call(
        pair_kernel,
        grid=(tiles,),
        in_specs=[
            split,
            split,
            back_row(wide3),
            back_row(wide3),
            once((8, wide)),
            once((1, dim)),
            once((4, wide)),
        ]
        + [ANYWHERE] * (len(shared) + len(after)),
        out_specs=[
            back_row(wide),
            whole_spec((4, wide)),
            whole_spec((1, wide)),
            whole_spec(TOKEN.shape),
        ],
        out_shape=[
            jax.ShapeDtypeStruct((seqs * width, wide), bf16),
            jax.ShapeDtypeStruct((4, wide), f32),
            jax.ShapeDtypeStruct((1, wide), f32),
            TOKEN,
        ],
        input_output_aliases={len(operands) + n: n for n in range(len(shared))},
        scratch_shapes=[pltpu.VMEM((8, wide), f32)],
        compiler_params=pltpu.CompilerParams(vmem_limit_bytes=60 * MIB),
        cost_estimate=lasting(11),
    )(*operands, *shared, *after)


def input_kernel(first_ref, rest_ref, x_ref, resid_ref, gain, w_ref, *refs):
    igrad_ref, d_gain, d_shift, token = refs[-4:]
    dim = x_ref.shape[1]
    token[...] = jnp.zeros_like(token)

    @pl.when(pl.program_id(0) == 0)
    def _():
        d_gain[...] = jnp.zeros_like(d_gain)
        d_shift[...] = jnp.zeros_like(d_shift)

    grad = dot_t(first_ref[...], w_ref[:, :dim]) + dot_t(rest_ref[...], w_ref[:, dim:])
    xhat, root = normalized(x_ref[...].astype(f32))
    d_shift[...] += column_sum(grad)
    d_gain[...] += column_sum(grad * xhat)
    igrad_ref[...] = resid_ref[...] + norm_back(grad, gain[...], xhat, root)


def input_grads(s, first, rest, inputs, resid, gain, weight, shared, after):
    seqs, width, dim = inputs.shape
    wide = weight.shape[1]
    tile = min(256, width)
    tiles = width // tile
    stacked = lambda cols: pl.BlockSpec((tile, cols), lambda i: (s * tiles + i, 0))
    layer = pl.BlockSpec((None, tile, dim), lambda i: (s, i, 0))
    operands = (first, rest, inputs, resid, gain, weight)
    return pl.pallas_call(
        input_kernel,
        grid=(tiles,),
        in_specs=[
            stacked(dim),
            stacked(wide - dim),
            layer,
            stacked(dim),
            once((1, dim)),
            once((dim, wide)),
        ]
        + [ANYWHERE] * (len(shared) + len(after)),
        out_specs=[layer, whole_spec((1, dim)), whole_spec((1, dim)), whole_spec(TOKEN.shape)],
        out_shape=[
            jax.ShapeDtypeStruct((seqs, width, dim), f32),
            jax.ShapeDtypeStruct((1, dim), f32),
            jax.ShapeDtypeStruct((1, dim), f32),
            TOKEN,
        ],
        input_output_aliases={len(operands) + n: n for n in range(len(shared))},
        compiler_params=pltpu.CompilerParams(vmem_limit_bytes=60 * MIB),
        cost_estimate=lasting(14),
    )(*operands, *shared, *after)


def over_tokens(left, right):
    return lax.dot_general(left, right, (((0,), (0,)), ((), ())), preferred_element_type=f32)


def tall_kernel(left, right, *refs):
    out, token = refs[-2:]
    token[...] = jnp.zeros_like(token)
    total = over_tokens(left[...], right[...])
    rows = out.shape[3]
    for b in range(out.shape[1]):
        out[0, b, 0] = total[b * rows : (b + 1) * rows].astype(bf16)


def flat_kernel(left, right, *refs):
    out, token = refs[-2:]
    token[...] = jnp.zeros_like(token)
    total = over_tokens(left[...], right[...])
    cores, buckets, zs, rows, _ = out.shape
    for z in range(zs):
        for c in range(cores):
            for b in range(buckets):
                at = ((cores * z + c) * buckets + b) * rows
                out[c, b, z] = total[at : at + rows].astype(bf16)


def two_kernel(steps, left, right, left2, right2, *refs):
    i = pl.program_id(0)

    @pl.when(i < steps)
    def _():
        flat_kernel(left, right, *refs)

    @pl.when(i >= steps)
    def _():
        flat_kernel(left2, right2, *refs)


def two_weight_grads(left, right, left2, right2, parts, buckets, after):
    tok, high = left.shape
    cols = right.shape[1]
    rows = high // parts // buckets
    if rows % 32:
        one, _ = weight_grad(left, right, parts, buckets, after)
        two, _ = weight_grad(left2, right2, parts, buckets, after)
        return jnp.concatenate([one, two], axis=1), after[0]
    block = min(512, cols)
    steps = cols // block
    shape = (2, buckets, parts // 2, rows, 2 * cols)
    total, token = pl.pallas_call(
        functools.partial(two_kernel, steps),
        grid=(2 * steps,),
        in_specs=[
            once((tok, high)),
            pl.BlockSpec((tok, block), lambda i: (0, jnp.minimum(i, steps - 1))),
            once((tok, high)),
            pl.BlockSpec((tok, block), lambda i: (0, jnp.maximum(i - steps, 0))),
        ]
        + [ANYWHERE] * len(after),
        out_specs=[
            pl.BlockSpec(shape[:4] + (block,), lambda i: (0, 0, 0, 0, i)),
            whole_spec(TOKEN.shape),
        ],
        out_shape=[jax.ShapeDtypeStruct(shape, bf16), TOKEN],
        compiler_params=pltpu.CompilerParams(vmem_limit_bytes=60 * MIB),
        cost_estimate=lasting(18),
    )(left, right, left2, right2, *after)
    return total.reshape(high, 2 * cols), token


def weight_grad(left, right, parts, buckets, after):
    tok, high = left.shape
    cols = right.shape[1]
    share = high // parts
    rows = share // buckets
    shape = (2, buckets, parts // 2, rows, cols)
    if rows % 32:
        total = jnp.einsum("tk,tn->kn", left, right, preferred_element_type=f32).astype(bf16)
        total = total.reshape(parts // 2, 2, buckets, rows, cols)
        return jnp.transpose(total, (1, 2, 0, 3, 4)).reshape(high, cols), after[0]
    tall = share % 512 == 0
    block = min(512, cols)
    if tall:
        steps = parts
        specs = [pl.BlockSpec((tok, share), lambda i: (0, i)), once((tok, cols))]
        out = pl.BlockSpec((1, buckets, 1, rows, cols), lambda i: (i % 2, 0, i // 2, 0, 0))
    else:
        steps = cols // block
        specs = [once((tok, high)), pl.BlockSpec((tok, block), lambda i: (0, i))]
        out = pl.BlockSpec(shape[:4] + (block,), lambda i: (0, 0, 0, 0, i))
    total, token = pl.pallas_call(
        tall_kernel if tall else flat_kernel,
        grid=(steps,),
        in_specs=specs + [ANYWHERE] * len(after),
        out_specs=[out, whole_spec(TOKEN.shape)],
        out_shape=[jax.ShapeDtypeStruct(shape, bf16), TOKEN],
        compiler_params=pltpu.CompilerParams(vmem_limit_bytes=60 * MIB),
        cost_estimate=lasting(23),
    )(left, right, *after)
    return total.reshape(high, cols), token


def swapped(block, axis, groups=None):
    return lax.all_to_all(
        block, axis, split_axis=0, concat_axis=0, tiled=True, axis_index_groups=groups
    )


def added(block):
    total = block[0].astype(f32)
    for n in range(1, block.shape[0]):
        total = total + block[n].astype(f32)
    return total


def tied(block, token):
    return block + (token[0, 0] * 0.0).astype(block.dtype)


def launch_kernel(*refs):
    refs[-1][...] = jnp.zeros_like(refs[-1])


def launched(block, after):
    return pl.pallas_call(
        launch_kernel,
        in_specs=[ANYWHERE] * (1 + len(after)),
        out_specs=[ANYWHERE, pl.BlockSpec(memory_space=pltpu.VMEM)],
        out_shape=[jax.ShapeDtypeStruct(block.shape, block.dtype), TOKEN],
        input_output_aliases={0: 0},
        cost_estimate=lasting(1),
    )(block, *after)


def pair_groups(parts):
    return [[2 * z, 2 * z + 1] for z in range(parts // 2)]


def pair_sum(block, parts):
    return lax.psum_scatter(
        block, "seq", scatter_dimension=0, tiled=True, axis_index_groups=pair_groups(parts)
    )


def bucket_sum(block):
    return lax.psum_scatter(block, "bucket", scatter_dimension=0, tiled=True)


def pair_swap(block, parts):
    block = block.reshape(2, -1, block.shape[1])
    return added(swapped(block, "seq", pair_groups(parts))).astype(bf16)


def bucket_swap(block, buckets):
    block = block.reshape(buckets, -1, block.shape[1])
    return added(swapped(block, "bucket")).astype(bf16)


def line_sum(block, parts):
    lines = [[2 * z + c for z in range(parts // 2)] for c in range(2)]
    block = block.reshape(parts // 2, -1, block.shape[1])
    return added(swapped(block, "seq", lines)).astype(bf16)


def gathered(block):
    return lax.all_gather(block, "bucket", axis=0, tiled=True).astype(f32)


def shared_out(block, buckets):
    cols = block.shape[1]
    block = swapped(jnp.broadcast_to(block, (buckets,) + block.shape), "bucket")
    return block.reshape(-1, cols).astype(f32)


def on_device(
    inputs,
    cotangent,
    lengths,
    norm_gains,
    norm_biases,
    in_weight,
    in_bias,
    short_conv,
    long_skip,
    filter_in,
    filter_mid,
    filter_vecs,
    filter_out,
    decay,
    out_weight,
    out_bias,
    up_weight,
    up_bias,
    down_weight,
    down_bias,
):
    seqs, width, dim = inputs.shape
    parts = lax.axis_size("seq")
    index = lax.axis_index("seq")
    chans = dim // parts
    fits = chans % LANES == 0
    blocks = parts if fits else 1
    row = lambda v: v.reshape(1, -1)
    gain1, gain2 = norm_gains[0:1], norm_gains[1:2]
    shift1, shift2 = norm_biases[0:1], norm_biases[1:2]
    skip = row(long_skip)
    tables = transform_tables()

    def to_channels(block):
        if not fits:
            block = jnp.swapaxes(block.reshape(width, parts, chans), 0, 1)
        got = lax.all_to_all(block, "seq", split_axis=0, concat_axis=0, tiled=True)
        got = got.reshape(LEN, chans)
        return got if fits else jnp.pad(got, ((0, 0), (0, LANES - chans)))

    def to_positions(block):
        block = block[:, :chans].reshape(parts, width, chans)
        got = lax.all_to_all(block, "seq", split_axis=0, concat_axis=0, tiled=True)
        return got if fits else jnp.swapaxes(got, 0, 1).reshape(1, width, dim)

    rims = passed_along(inputs[:, width - 2 :, :], "seq", 1)
    rims = jnp.pad(rims, ((0, 0), (14, 0), (0, 0)))
    flag = (index > 0).astype(f32).reshape(1, 1)
    counts = jnp.clip(lengths - index * width, 0, width)

    buckets = lax.axis_size("bucket")

    data, carried = [], []
    shared = ()
    for s in range(seqs):
        got = front(s, inputs, rims, flag, gain1, shift1, in_weight, row(in_bias), short_conv,
                    blocks, shared)
        shared, token = got[:3], got[4]
        carried.append(got[3])
        data.append(to_channels(got[3]))
    normed, proj, mixed = shared

    start = index * chans
    columns = lax.dynamic_slice_in_dim(filter_out, start, chans, 1)
    rates = lax.dynamic_slice_in_dim(decay, start, chans, 0)

    def make_taps(first_w, mid_w, vecs, cols):
        return filter_taps(first_w, mid_w, vecs, cols, rates)

    taps, taps_pull = jax.vjp(make_taps, filter_in, filter_mid, filter_vecs, columns)
    taps_spec = taps_transform(
        taps if fits else jnp.pad(taps, ((0, 0), (0, LANES - chans))), tables, (data[0],)
    )

    specs, convs = [], []
    for s in range(seqs):
        conv, spec, token = long_conv(data[s], taps_spec, tables, None, (token,))
        specs.append(spec)
        convs.append(to_positions(conv))

    mid_sums, grad_convs, grads = [], [], []
    shared = ()
    for s in range(seqs):
        got = middle(
            s, counts[s : s + 1], convs[s], carried[s], mixed, inputs, cotangent, skip, gain2,
            shift2, out_weight, row(out_bias), up_weight, row(up_bias), down_weight,
            row(down_bias), shared, (token,),
        )
        shared, token = got[:9], got[10]
        mid_sums.append(got[10:])
        grad_convs.append(got[9])
        grads.append(to_channels(got[9]))
    output, act, grad_hidden, normed2, gated, grad_down_in, grad_branch, resid, grad_gate = shared

    up, token = weight_grad(normed2, grad_hidden, parts, buckets, (token, grads[0]))
    down, token = weight_grad(act, grad_down_in, parts, buckets, (token,))
    up, token = launched(up, (token, grads[-1]))
    up = pair_sum(up, parts)
    down, token = launched(down, (token,))
    down = pair_sum(down, parts)

    gate_rims = tied(grad_gate.reshape(seqs, width, dim)[:, :2], token)
    gate_rims = passed_along(gate_rims, "seq", -1).astype(f32)
    gate_rims = jnp.pad(gate_rims, ((0, 0), (0, 6), (0, 0)))

    corrs, gbacks = [], []
    for s in range(seqs):
        back, corr, token = long_conv(grads[s], taps_spec, tables, specs[s], (token,))
        if s == 0:
            up, token = launched(up, (token,))
            up = bucket_sum(up)
        corrs.append(corr)
        gbacks.append(to_positions(back))
    grad_first, d_short1, d_bias1, token = gate_grads(
        seqs, grad_gate, proj, gate_rims, short_conv[:, :dim], (token,)
    )
    both, token = two_weight_grads(
        gated, grad_branch, normed, grad_first, parts, buckets, (token,)
    )
    down, token = launched(down, (token, gbacks[0], up))
    down = bucket_sum(down)
    both, token = launched(both, (token,))
    both = pair_sum(both, parts)

    def first_rows(block):
        return jnp.swapaxes(block[:, :2], 0, 1).reshape(2, dim).astype(f32)

    grad_taps, token = taps_back(corrs, tables, (token,))
    d_fin, d_fmid, d_fvecs, d_cols = taps_pull(grad_taps[:, :chans])

    rim_rows = []
    for s in range(seqs):
        grad_carried = first_rows(gbacks[s]) + skip * first_rows(grad_convs[s])
        edge = mixed[s * width : s * width + 2].astype(f32)
        rim_rows.append(
            jnp.concatenate(
                [grad_carried * edge[:, 2 * dim :], grad_carried * edge[:, dim : 2 * dim]], axis=1
            )
        )
    rim = passed_along(tied(jnp.stack(rim_rows), d_fin), "seq", -1)
    rim = jnp.pad(rim, ((0, 0), (0, 6), (0, 0)))
    pair_sums = []
    shared = ()
    both, token = launched(both, (token, d_fin, d_cols, gbacks[-1]))
    both = bucket_sum(both)
    up, token = launched(up, (token,))
    up = line_sum(up, parts)
    hold = ()
    for s in range(seqs):
        got = pair_grads(s, seqs, gbacks[s], grad_convs[s], mixed, proj, rim[s], skip,
                         short_conv[:, dim:], shared, (token,) + hold)
        hold = (up,)
        shared, token = got[:1], got[3]
        pair_sums.append(got[1:3])
    grad_rest = shared[0]
    down = line_sum(down, parts)
    rest, token = weight_grad(normed, grad_rest, parts, buckets, (token, down))
    rest = pair_swap(rest, parts)
    rest = bucket_swap(rest, buckets)
    end_sums = []
    shared = ()
    hold = ()
    for s in range(seqs):
        got = input_grads(s, grad_first, grad_rest, inputs, resid, gain1, in_weight, shared,
                          (token,) + hold)
        shared, token = got[:1], got[3]
        end_sums.append(got[1:3])
        hold = (both,)
    d_up_weight = gathered(up)
    d_down_weight = gathered(down)
    last = line_sum(jnp.concatenate([both, rest], axis=1), parts)
    last = shared_out(last, buckets)
    d_out_weight, d_in_weight = last[:, :dim], last[:, dim:]
    input_grad = shared[0]

    def summed(lists, n):
        total = lists[0][n]
        for other in lists[1:]:
            total = total + other[n]
        return total

    small = [
        jnp.concatenate([summed(end_sums, 0), summed(mid_sums, 0)], axis=0),
        jnp.concatenate([summed(end_sums, 1), summed(mid_sums, 1)], axis=0),
        jnp.concatenate([d_bias1, summed(pair_sums, 1)], axis=1),
        jnp.concatenate([d_short1, summed(pair_sums, 0)], axis=1),
        summed(mid_sums, 5),
        d_fin,
        d_fmid,
        d_fvecs,
        summed(mid_sums, 4),
        summed(mid_sums, 3),
        summed(mid_sums, 2),
    ]
    flat = jnp.concatenate(
        [
            jnp.swapaxes(piece.reshape(piece.shape[0], parts, -1), 0, 1).reshape(parts, -1)
            for piece in small
        ],
        axis=1,
    )
    flat = added(swapped(flat, "seq"))
    flat = jnp.concatenate([flat, d_cols.reshape(-1)])
    flat = added(swapped(jnp.broadcast_to(flat, (buckets,) + flat.shape), "bucket"))
    shares = []
    at = 0
    for shape in [piece.shape for piece in small] + [d_cols.shape]:
        share = shape[1] if len(shares) == len(small) else shape[1] // parts
        shares.append(flat[at : at + shape[0] * share].reshape(shape[0], share))
        at += shape[0] * share
    (d_gains, d_shifts, d_in_bias, d_short, d_skip, d_fin, d_fmid, d_fvecs, d_out_b, d_up_b,
     d_down_b, d_fout) = shares

    return (
        output,
        input_grad,
        d_gains,
        d_shifts,
        d_in_weight,
        d_in_bias.reshape(-1),
        d_short,
        d_skip.reshape(-1),
        d_fin,
        d_fmid,
        d_fvecs,
        d_fout,
        d_out_weight,
        d_out_b.reshape(-1),
        d_up_weight,
        d_up_b.reshape(-1),
        d_down_weight,
        d_down_b.reshape(-1),
    )


def solution(mesh):
    whole = P()
    in_specs = (P("bucket", "seq", None),) * 2 + (P("bucket"),) + (whole,) * 17
    rows, cols, flat = P("seq", None), P(None, "seq"), P("seq")
    out_specs = (
        P("bucket", "seq", None),
        P("bucket", "seq", None),
        cols,
        cols,
        rows,
        flat,
        cols,
        flat,
        cols,
        cols,
        cols,
        cols,
        rows,
        flat,
        rows,
        flat,
        rows,
        flat,
    )
    return jax.shard_map(
        on_device, mesh=mesh, in_specs=in_specs, out_specs=out_specs, check_vma=False
    )
```

```python
import functools
import math

import jax
import jax.numpy as jnp
import ml_dtypes
import numpy as np
from jax import lax
from jax.experimental import pallas as pl
from jax.experimental.pallas import tpu as pltpu
from jax.sharding import PartitionSpec as P

EMB = 33
LEN = 8192
HALF = 64
KB = 128
LANES = 128
STEP_K = 32
STEP_F = 8
ROWS_K = KB + 1
ROWS_F = 2 * KB + 1
ROWS_E = 48
MID_TILE = 256
MID_BLOCK = 512

epsilon = 1e-05
f32 = jnp.float32
bf16 = jnp.bfloat16
MIB = 2**20


def lasting(micros):
    return pl.CostEstimate(
        flops=int(micros * 1.1e9), bytes_accessed=1000, transcendentals=0
    )


def passed_along(block, axis, distance):
    devices = range(lax.axis_size(axis))
    route = [(i - distance, i) for i in devices if i - distance in devices]
    return lax.ppermute(block, axis, route)


def dot(left, right):
    return jnp.dot(left, right, preferred_element_type=f32)


def dot_t(left, right):
    return lax.dot_general(left, right, (((1,), (1,)), ((), ())), preferred_element_type=f32)


def positions_table():
    steps = np.arange(LEN)
    bands = np.arange((EMB - 1) // 2)
    angle = 2.0 * np.pi * (bands[:, None] * steps[None, :] % LEN) / LEN
    first = steps[None, :] / (LEN - 1)
    table = np.concatenate([first, np.cos(angle), -np.sin(angle)], axis=0)
    return jnp.asarray(np.pad(table, ((0, ROWS_E - EMB), (0, 0))).astype(np.float32))


def halves(block):
    high = block.astype(bf16)
    return high, (block - high.astype(f32)).astype(bf16)


def exact(left, right, contract):
    high, low = halves(left)
    left = jnp.concatenate([high, high, low], axis=contract[0][0])
    high, low = halves(right)
    right = jnp.concatenate([high, low, high], axis=contract[1][0])
    return lax.dot_general(left, right, (contract, ((), ())), preferred_element_type=f32)


def sine_series(r):
    square = r * r
    poly = -1.0 / 39916800.0
    for term in (1.0 / 362880.0, -1.0 / 5040.0, 1.0 / 120.0, -1.0 / 6.0):
        poly = poly * square + term
    return r + r * square * poly


def without_turns(x, n):
    return x - n * 3.140625 - n * 9.67502593994140625e-4 - n * 1.509957990978376432e-7


def sign_of(n):
    return 1.0 - 2.0 * (n.astype(jnp.int32) & 1).astype(f32)


def sine(x):
    n = jnp.floor(x * (1.0 / math.pi) + 0.5)
    return sign_of(n) * sine_series(without_turns(x, n))


def cosine(x):
    n = jnp.floor(x * (1.0 / math.pi))
    return -sign_of(n) * sine_series(without_turns(x, n + 0.5))


CHUNK = 1024


def filter_layers(emb, w_in, w_mid, vecs):
    bias1, freq1, bias2, freq2 = (vecs[:, n : n + 1] for n in range(4))
    at1 = exact(w_in, emb, ((1,), (0,))) + bias1
    first = sine(freq1 * at1)
    at2 = exact(w_mid, first, ((1,), (0,))) + bias2
    return at1, first, at2


def window(first, rates):
    steps = (first + lax.broadcasted_iota(jnp.int32, (KB, LANES), 0)).astype(f32)
    return jnp.exp(-rates * steps)


def transform_tables():
    m = np.arange(HALF)
    k = np.arange(KB)
    f = np.arange(HALF)
    turns = ((4 * f[None, :, None] + 1) * (KB * m[None, None, :] + k[:, None, None])) % (4 * LEN)
    phase = 2 * np.pi * turns / (4 * LEN)
    table = np.concatenate([np.cos(phase), -np.sin(phase)], axis=1).astype(np.float32)
    high = table.astype(ml_dtypes.bfloat16)
    low = (table - high.astype(np.float32)).astype(ml_dtypes.bfloat16)
    onward = np.concatenate([high, low], axis=2)
    back = np.ascontiguousarray(np.swapaxes(table, 1, 2)).astype(ml_dtypes.bfloat16)
    angle = 2 * np.pi * ((k[:, None] * k[None]) % KB) / KB
    cos, sin = np.cos(angle), np.sin(angle)
    inner = np.block([[cos, sin], [-sin, cos]])
    return (
        jnp.asarray(onward),
        jnp.asarray(back),
        jnp.asarray(inner.astype(ml_dtypes.bfloat16)),
        jnp.asarray(np.ascontiguousarray(inner.T).astype(ml_dtypes.bfloat16)),
    )


def looped(count, unroll, body):
    def step(i, carry):
        for u in range(unroll):
            body(i * unroll + u)
        return carry

    lax.fori_loop(0, count // unroll, step, 0)


def fetch(src, dst, sems, first, pieces):
    rows = dst.shape[0] // pieces
    copies = []
    for n in range(pieces):
        part = pl.ds(n * rows, rows)
        copy = pltpu.make_async_copy(src.at[part], dst.at[part], sems.at[first + n])
        copy.start()
        copies.append(copy)
    return copies


def outer_stage(first, count, exact, src, table, dst):
    def body(n):
        k = first + n
        rows = src[pl.ds(k, HALF, stride=ROWS_K), :]
        high = rows.astype(bf16)
        out = dot(table[k], jnp.concatenate([high, high], axis=0))
        if not exact:
            low = (rows - high.astype(f32)).astype(bf16)
            out = out + dot(table[k, :, :HALF], low)
        dst[pl.ds(k, HALF, stride=ROWS_F), :] = out[:HALF]
        dst[pl.ds(k + KB, HALF, stride=ROWS_F), :] = out[HALF:]

    looped(count, STEP_K, body)


def outer_back(first, count, src, table, dst):
    def body(n):
        k = first + n
        real = src[pl.ds(k, HALF, stride=ROWS_F), :]
        imag = src[pl.ds(k + KB, HALF, stride=ROWS_F), :]
        rows = jnp.concatenate([real, imag], axis=0).astype(bf16)
        dst[pl.ds(k, HALF, stride=ROWS_K), :] = dot(table[k], rows)

    looped(count, STEP_K, body)


def spaced(src, dst, first, count):
    for m in range(first, first + count):
        dst[m * ROWS_K : m * ROWS_K + KB] = src[m * KB : (m + 1) * KB].astype(f32)


def packed(src, dst):
    for m in range(HALF):
        rows = src[m * ROWS_K : m * ROWS_K + KB] * (1.0 / LEN)
        dst[m * KB : (m + 1) * KB] = rows.astype(bf16)


def row_pair(at):
    row = at * (2 * ROWS_F)
    return pl.ds(row, 2 * KB), pl.ds(row + ROWS_F, 2 * KB)


PIECES = 4


def conv_kernel(backward, x_ref, h_ref, *refs):
    if backward:
        spec_in, *refs = refs
    ta_ref, tai_ref, tb, tbi = refs[:4]
    y_ref, spec_ref, token, x, h, spec, ta, tai, xs, mid, sems = refs[-11:]
    token[...] = jnp.zeros_like(token)
    x_in = fetch(x_ref, x, sems, 0, 2)
    ta_in = fetch(ta_ref, ta, sems, 2, PIECES)
    h_in = fetch(h_ref, h, sems, 2 + PIECES, PIECES)
    s_in = fetch(spec_in, spec, sems, 2 + 2 * PIECES, PIECES) if backward else ()
    tai_in = fetch(tai_ref, tai, sems, 2 + 3 * PIECES, 1)
    half = HALF // 2
    for n in range(2):
        x_in[n].wait()
        spaced(x, xs, n * half, half)
    for n in range(PIECES):
        ta_in[n].wait()
        outer_stage(n * KB // PIECES, KB // PIECES, True, xs, ta, mid)

    def inner(first):
        def body(n):
            at = first + n
            left, right = row_pair(at)
            both = jnp.concatenate([mid[left, :].astype(bf16), mid[right, :].astype(bf16)], axis=1)
            freq = dot(tb[...], both)
            prods = []
            for v in range(2):
                f = 2 * at + v
                re = freq[:KB, v * LANES : (v + 1) * LANES]
                im = freq[KB:, v * LANES : (v + 1) * LANES]
                hr = h[f, :KB].astype(f32)
                hi = h[f, KB:].astype(f32)
                if backward:
                    pr, pi = re * hr + im * hi, im * hr - re * hi
                    sr = spec[f, :KB].astype(f32)
                    si = spec[f, KB:].astype(f32)
                    spec[f, :KB] = (re * sr + im * si).astype(bf16)
                    spec[f, KB:] = (im * sr - re * si).astype(bf16)
                else:
                    pr, pi = re * hr - im * hi, re * hi + im * hr
                    spec[f, :KB] = re.astype(bf16)
                    spec[f, KB:] = im.astype(bf16)
                prods.append(jnp.concatenate([pr, pi], axis=0).astype(bf16))
            out = dot(tbi[...], jnp.concatenate(prods, axis=1))
            mid[left, :] = out[:, :LANES]
            mid[right, :] = out[:, LANES:]

        return body

    leaving = []
    rows = HALF // PIECES
    for n in range(PIECES):
        h_in[n].wait()
        if backward:
            s_in[n].wait()
        looped(rows // 2, STEP_F, inner(n * rows // 2))
        part = pl.ds(n * rows, rows)
        copy = pltpu.make_async_copy(spec.at[part], spec_ref.at[part], sems.at[3 + 3 * PIECES + n])
        copy.start()
        leaving.append(copy)
    tai_in[0].wait()
    outer_back(0, KB, mid, tai, xs)
    packed(xs, y_ref)
    for copy in leaving:
        copy.wait()


def whole_spec(shape):
    return pl.BlockSpec(shape, lambda i: (0,) * len(shape))


def once(shape):
    return pl.BlockSpec(shape, lambda i: (0,) * len(shape), pipeline_mode=pl.Buffered(1))


TOKEN = jax.ShapeDtypeStruct((8, LANES), f32)
ANYWHERE = pl.BlockSpec(memory_space=pl.ANY)
IN_VMEM = pl.BlockSpec(memory_space=pltpu.VMEM)
SPECTRUM = (HALF, 2 * KB, LANES)


def long_conv(rows, taps_spec, tables, data_spec=None, after=()):
    backward = data_spec is not None
    onward, back, inner, inner_back = tables
    extra = [data_spec] if backward else []
    return pl.pallas_call(
        functools.partial(conv_kernel, backward),
        in_specs=[ANYWHERE] * (4 + len(extra)) + [IN_VMEM] * 2 + [ANYWHERE] * len(after),
        out_specs=[IN_VMEM, ANYWHERE, IN_VMEM],
        out_shape=[
            jax.ShapeDtypeStruct((LEN, LANES), bf16),
            jax.ShapeDtypeStruct(SPECTRUM, bf16),
            TOKEN,
        ],
        scratch_shapes=[
            pltpu.VMEM((LEN, LANES), bf16),
            pltpu.VMEM(SPECTRUM, bf16),
            pltpu.VMEM(SPECTRUM, bf16),
            pltpu.VMEM(onward.shape, bf16),
            pltpu.VMEM(back.shape, bf16),
            pltpu.VMEM((HALF * ROWS_K, LANES), f32),
            pltpu.VMEM((HALF * ROWS_F, LANES), f32),
            pltpu.SemaphoreType.DMA((3 + 4 * PIECES,)),
        ],
        compiler_params=pltpu.CompilerParams(vmem_limit_bytes=60 * MIB),
        cost_estimate=lasting(14),
    )(rows, taps_spec, *extra, onward, back, inner, inner_back, *after)


def taps_kernel(emb, w_in, w_mid, vecs, cols, rates, ta_ref, tb, *refs):
    h_ref, ta, xs, mid, h, sems = refs[-6:]
    ta_in = fetch(ta_ref, ta, sems, 0, PIECES)

    def chunk(c, carry):
        part = pl.ds(pl.multiple_of(c * CHUNK, CHUNK), CHUNK)
        _, _, at2 = filter_layers(emb[:, part], w_in[...], w_mid[...], vecs)
        second = sine(vecs[:, 3:4] * at2)
        taps = exact(second, cols[...], ((0,), (0,)))
        for n in range(CHUNK // KB):
            m = c * (CHUNK // KB) + n
            xs[pl.ds(m * ROWS_K, KB), :] = taps[n * KB : (n + 1) * KB] * window(m * KB, rates[...])
        return carry

    lax.fori_loop(0, LEN // CHUNK, chunk, 0)
    for n in range(PIECES):
        ta_in[n].wait()
        outer_stage(n * KB // PIECES, KB // PIECES, False, xs, ta, mid)

    def body(at):
        left, right = row_pair(at)
        both = jnp.concatenate([mid[left, :].astype(bf16), mid[right, :].astype(bf16)], axis=1)
        freq = dot(tb[...], both)
        h[2 * at] = freq[:, :LANES].astype(bf16)
        h[2 * at + 1] = freq[:, LANES:].astype(bf16)

    leaving = []
    rows = HALF // PIECES
    for n in range(PIECES):
        looped(rows // 2, STEP_F, lambda at, n=n: body(n * rows // 2 + at))
        part = pl.ds(n * rows, rows)
        copy = pltpu.make_async_copy(h.at[part], h_ref.at[part], sems.at[PIECES + n])
        copy.start()
        leaving.append(copy)
    for copy in leaving:
        copy.wait()


def taps_transform(network, tables, after):
    onward, _, inner, _ = tables
    return pl.pallas_call(
        taps_kernel,
        in_specs=[IN_VMEM] * 6 + [ANYWHERE, IN_VMEM] + [ANYWHERE] * len(after),
        out_specs=ANYWHERE,
        out_shape=jax.ShapeDtypeStruct(SPECTRUM, bf16),
        scratch_shapes=[
            pltpu.VMEM(onward.shape, bf16),
            pltpu.VMEM((HALF * ROWS_K, LANES), f32),
            pltpu.VMEM((HALF * ROWS_F, LANES), f32),
            pltpu.VMEM(SPECTRUM, bf16),
            pltpu.SemaphoreType.DMA((2 * PIECES,)),
        ],
        compiler_params=pltpu.CompilerParams(vmem_limit_bytes=60 * MIB),
        cost_estimate=lasting(15),
    )(*network, onward, inner, *after)


def taps_back_kernel(count, *refs):
    specs = refs[:count]
    tai_ref, tbi, emb, w_in, w_mid, vecs, cols, rates = refs[count : count + 8]
    d_in, d_mid, d_vecs, d_cols, token, tai, mid, ys, held, sems = refs[-10:]
    token[...] = jnp.zeros_like(token)
    tai_in = fetch(tai_ref, tai, sems, 0, 1)
    arrivals = [
        fetch(specs[c], held.at[c], sems, 1 + c * PIECES, PIECES) for c in range(count)
    ]

    def body(at):
        left, right = row_pair(at)
        prods = []
        for v in range(2):
            total = held[0, 2 * at + v].astype(f32)
            for c in range(1, count):
                total = total + held[c, 2 * at + v].astype(f32)
            prods.append(total.astype(bf16))
        out = dot(tbi[...], jnp.concatenate(prods, axis=1))
        mid[left, :] = out[:, :LANES]
        mid[right, :] = out[:, LANES:]

    rows = HALF // PIECES
    for n in range(PIECES):
        for c in range(count):
            arrivals[c][n].wait()
        looped(rows // 2, STEP_F, lambda at, n=n: body(n * rows // 2 + at))
    tai_in[0].wait()
    outer_back(0, KB, mid, tai, ys)
    for ref in (d_in, d_mid, d_vecs, d_cols):
        ref[...] = jnp.zeros_like(ref)

    def chunk(c, carry):
        part = pl.ds(pl.multiple_of(c * CHUNK, CHUNK), CHUNK)
        at1, first, at2 = filter_layers(emb[:, part], w_in[...], w_mid[...], vecs)
        freq1, freq2 = vecs[:, 1:2], vecs[:, 3:4]
        second = sine(freq2 * at2)
        rows = []
        for n in range(CHUNK // KB):
            m = c * (CHUNK // KB) + n
            rows.append(ys[pl.ds(m * ROWS_K, KB), :] * (window(m * KB, rates[...]) * (1.0 / LEN)))
        grad = jnp.concatenate(rows, axis=0)
        d_cols[...] += exact(second, grad, ((1,), (0,)))
        turn2 = exact(cols[...], grad, ((1,), (1,))) * cosine(freq2 * at2)
        inner2 = turn2 * freq2
        d_mid[...] += exact(first, inner2, ((1,), (1,)))
        turn1 = exact(w_mid[...], inner2, ((0,), (0,))) * cosine(freq1 * at1)
        inner1 = turn1 * freq1
        d_in[...] += exact(emb[:, part], inner1, ((1,), (1,)))
        for n, terms in enumerate((inner1, turn1 * at1, inner2, turn2 * at2)):
            d_vecs[:, n : n + 1] += jnp.sum(terms, axis=1, keepdims=True)
        return carry

    lax.fori_loop(0, LEN // CHUNK, chunk, 0)


def taps_back(specs, tables, network, after):
    _, back, _, inner_back = tables
    count = len(specs)
    hidden = network[2].shape[0]
    return pl.pallas_call(
        functools.partial(taps_back_kernel, count),
        in_specs=[ANYWHERE] * (count + 1) + [IN_VMEM] * 7 + [ANYWHERE] * len(after),
        out_specs=[IN_VMEM] * 5,
        out_shape=[
            jax.ShapeDtypeStruct((ROWS_E, hidden), f32),
            jax.ShapeDtypeStruct((hidden, hidden), f32),
            jax.ShapeDtypeStruct((hidden, 4), f32),
            jax.ShapeDtypeStruct((hidden, LANES), f32),
            TOKEN,
        ],
        scratch_shapes=[
            pltpu.VMEM(back.shape, bf16),
            pltpu.VMEM((HALF * ROWS_F, LANES), f32),
            pltpu.VMEM((HALF * ROWS_K, LANES), f32),
            pltpu.VMEM((count,) + SPECTRUM, bf16),
            pltpu.SemaphoreType.DMA((1 + count * PIECES,)),
        ],
        compiler_params=pltpu.CompilerParams(vmem_limit_bytes=60 * MIB),
        cost_estimate=lasting(20),
    )(*specs, back, inner_back, *network, *after)


def normalized(rows):
    mean = jnp.mean(rows, axis=-1, keepdims=True)
    centered = rows - mean
    spread = jnp.mean(centered * centered, axis=-1, keepdims=True)
    root = lax.rsqrt(spread + epsilon)
    return centered * root, root


def norm_back(grad, gain, xhat, root):
    g = grad * gain
    mean = jnp.mean(g, axis=-1, keepdims=True)
    along = jnp.mean(g * xhat, axis=-1, keepdims=True)
    return (g - mean - xhat * along) * root


def column_sum(block):
    return jnp.sum(block, axis=0, keepdims=True)


def joined(ref):
    if ref.shape[0] == 1:
        return ref[0]
    return jnp.concatenate([ref[b] for b in range(ref.shape[0])], axis=1)


def spread_out(ref, first, block):
    chans = ref.shape[2]
    width = block.shape[1]
    if chans >= first + width and ref.shape[0] == 1:
        ref[0, :, first : first + width] = block
        return
    for at in range(0, width, chans):
        ref[(first + at) // chans] = block[:, at : at + chans]


def front_kernel(
    x_ref, rim_ref, flag_ref, gain, shift, w_ref, b_ref, short, *refs
):
    normed_ref, proj_ref, mixed_ref, carried_ref, token, tail = refs[-6:]
    i = pl.program_id(0)
    tile, dim = x_ref.shape
    token[...] = jnp.zeros_like(token)

    @pl.when(i == 0)
    def _():
        rows, _ = normalized(rim_ref[...].astype(f32))
        rows = (rows * gain[...] + shift[...]).astype(bf16)
        edge = (dot(rows, w_ref[...]) + b_ref[...]).astype(bf16).astype(f32)
        tail[...] = edge[8:] * flag_ref[...]

    xhat, _ = normalized(x_ref[...].astype(f32))
    normed = (xhat * gain[...] + shift[...]).astype(bf16)
    normed_ref[...] = normed
    block = 256
    at_row = lax.broadcasted_iota(jnp.int32, (tile, block), 0)
    for first in range(0, dim, block):
        parts = []
        for stream in range(3):
            cols = slice(stream * dim + first, stream * dim + first + block)
            proj = (dot(normed, w_ref[:, cols]) + b_ref[:, cols]).astype(bf16)
            proj_ref[:, cols] = proj
            proj = proj.astype(f32)
            one = jnp.where(at_row == 0, tail[7:8, cols], pltpu.roll(proj, 1, 0))
            two = jnp.where(
                at_row == 0,
                tail[6:7, cols],
                jnp.where(at_row == 1, tail[7:8, cols], pltpu.roll(proj, 2, 0)),
            )
            mixed = (
                short[0:1, cols] * two
                + short[1:2, cols] * one
                + short[2:3, cols] * proj
                + short[3:4, cols]
            )
            mixed_ref[:, cols] = mixed.astype(bf16)
            tail[:, cols] = proj[tile - 8 :]
            parts.append(mixed)
        spread_out(carried_ref, first, (parts[1] * parts[2]).astype(bf16))


def front(s, inputs, rims, flag, gain, shift, weight, bias, short, blocks, shared, after):
    seqs, width, dim = inputs.shape
    tile = min(256, width)
    tiles = width // tile
    wide = weight.shape[1]
    tok = seqs * width
    stacked = lambda cols: pl.BlockSpec((tile, cols), lambda i: (s * tiles + i, 0))
    operands = (inputs, rims, flag, gain, shift, weight, bias, short)
    return pl.pallas_call(
        front_kernel,
        grid=(tiles,),
        in_specs=[
            pl.BlockSpec((None, tile, dim), lambda i: (s, i, 0)),
            pl.BlockSpec((None,) + rims.shape[1:], lambda i: (s, 0, 0)),
            once((1, 1)),
            once((1, dim)),
            once((1, dim)),
            once((dim, wide)),
            once((1, wide)),
            once((4, wide)),
        ]
        + [ANYWHERE] * (len(shared) + len(after)),
        out_specs=[
            stacked(dim),
            stacked(wide),
            stacked(wide),
            pl.BlockSpec((blocks, tile, dim // blocks), lambda i: (0, i, 0)),
            whole_spec(TOKEN.shape),
        ],
        out_shape=[
            jax.ShapeDtypeStruct((tok, dim), bf16),
            jax.ShapeDtypeStruct((tok, wide), bf16),
            jax.ShapeDtypeStruct((tok, wide), bf16),
            jax.ShapeDtypeStruct((blocks, width, dim // blocks), bf16),
            TOKEN,
        ],
        input_output_aliases={len(operands) + n: n for n in range(len(shared))},
        scratch_shapes=[pltpu.VMEM((8, wide), f32)],
        compiler_params=pltpu.CompilerParams(vmem_limit_bytes=60 * MIB),
        cost_estimate=lasting(20),
    )(*operands, *shared, *after)


def gelu_and_slope(hidden):
    size = jnp.abs(hidden)
    bell = jnp.exp(hidden * hidden * -0.5)
    t = pl.reciprocal(1.0 + size * (0.3275911 / math.sqrt(2.0)), approx=False)
    poly = 0.5 * 1.061405429
    for term in (-1.453152027, 1.421413741, -0.284496736, 0.254829592):
        poly = poly * t + 0.5 * term
    rest = poly * t * bell
    below = jnp.where(hidden >= 0, 1.0 - rest, rest)
    return hidden * below, below + hidden * (bell * (1.0 / math.sqrt(2.0 * math.pi)))


def mid_kernel(
    count_ref, conv_ref, carried_ref, gate_ref, x_ref, cot_ref, skip, gain, shift, w_out, b_out,
    w_up, b_up, w_down, b_down, *refs
):
    (
        out_ref, act_ref, gh_ref, normed_ref, gated_ref, gdi_ref, branch_ref, resid_ref, ggo_ref,
        gconv_ref, d_gain, d_shift, d_down_b, d_up_b, d_out_b, d_skip
    ) = refs[-16:]
    i = pl.program_id(0)
    tile, dim = x_ref.shape
    hid = w_up.shape[1]

    @pl.when(i == 0)
    def _():
        for ref in (d_gain, d_shift, d_down_b, d_up_b, d_out_b, d_skip):
            ref[...] = jnp.zeros_like(ref)

    place = i * tile + lax.broadcasted_iota(jnp.int32, (tile, 1), 0)
    mask = (place < count_ref[0]).astype(f32)
    carried = joined(carried_ref).astype(f32)
    gate = gate_ref[...].astype(f32)
    long_out = joined(conv_ref).astype(f32) + skip[...] * carried
    gated = (gate * long_out).astype(bf16)
    gated_ref[...] = gated
    resid = x_ref[...].astype(f32) + dot(gated, w_out[...]) + b_out[...]
    xhat, root = normalized(resid)
    normed = (xhat * gain[...] + shift[...]).astype(bf16)
    normed_ref[...] = normed
    grad_final = cot_ref[...].astype(f32) * mask
    gdi = grad_final.astype(bf16)
    gdi_ref[...] = gdi
    d_down_b[...] += column_sum(grad_final)
    final = resid + b_down[...]
    back = jnp.zeros((tile, dim), f32)
    block = MID_BLOCK
    for first in range(0, hid, block):
        cols = slice(first, first + block)
        hidden = dot(normed, w_up[:, cols]) + b_up[:, cols]
        grad_act = dot_t(gdi, w_down[cols, :])
        act, slope = gelu_and_slope(hidden)
        act = act.astype(bf16)
        grad_hidden = (slope * grad_act).astype(bf16)
        act_ref[:, cols] = act
        gh_ref[:, cols] = grad_hidden
        d_up_b[:, cols] += column_sum(grad_hidden.astype(f32))
        final = final + dot(act, w_down[cols, :])
        back = back + dot_t(grad_hidden, w_up[:, cols])
    out_ref[...] = (final * mask).astype(bf16)
    d_shift[...] += column_sum(back)
    d_gain[...] += column_sum(back * xhat)
    grad_resid = grad_final + norm_back(back, gain[...], xhat, root)
    resid_ref[...] = grad_resid
    branch = grad_resid.astype(bf16)
    branch_ref[...] = branch
    d_out_b[...] += column_sum(branch.astype(f32))
    grad_gated = dot_t(branch, w_out[...])
    ggo_ref[...] = (grad_gated * long_out).astype(bf16)
    grad_long = grad_gated * gate
    d_skip[...] += column_sum(grad_long * carried)
    spread_out(gconv_ref, 0, grad_long.astype(bf16))


def middle(s, count, conv, carried, mixed, inputs, cot, skip, gain, shift, w_out, b_out, w_up,
           b_up, w_down, b_down, shared, after):
    seqs, width, dim = inputs.shape
    hid = w_up.shape[1]
    blocks, _, chans = carried.shape
    tile = min(MID_TILE, width)
    tiles = width // tile
    split = pl.BlockSpec((blocks, tile, chans), lambda i: (0, i, 0))
    stacked = lambda cols: pl.BlockSpec((tile, cols), lambda i: (i + s * tiles, 0))
    layer = pl.BlockSpec((None, tile, dim), lambda i: (s, i, 0))
    tok = seqs * width
    sums = [dim, dim, dim, hid, dim, dim]
    shapes = [
        ((seqs, width, dim), bf16),
        ((tok, hid), bf16),
        ((tok, hid), bf16),
        ((tok, dim), bf16),
        ((tok, dim), bf16),
        ((tok, dim), bf16),
        ((tok, dim), bf16),
        ((tok, dim), f32),
        ((tok, dim), bf16),
        ((blocks, width, chans), bf16),
    ] + [((1, n), f32) for n in sums]
    operands = (count, conv, carried, mixed, inputs, cot, skip, gain, shift, w_out, b_out, w_up,
                b_up, w_down, b_down)
    aliases = {len(operands) + n: n for n in range(len(shared))}
    return pl.pallas_call(
        mid_kernel,
        grid=(tiles,),
        in_specs=[
            pl.BlockSpec(memory_space=pltpu.SMEM),
            split,
            split,
            stacked(dim),
            layer,
            layer,
            once((1, dim)),
            once((1, dim)),
            once((1, dim)),
            once((dim, dim)),
            once((1, dim)),
            once((dim, hid)),
            once((1, hid)),
            once((hid, dim)),
            once((1, dim)),
        ]
        + [ANYWHERE] * (len(shared) + len(after)),
        out_specs=[
            layer,
            stacked(hid),
            stacked(hid),
            stacked(dim),
            stacked(dim),
            stacked(dim),
            stacked(dim),
            stacked(dim),
            stacked(dim),
            split,
        ]
        + [whole_spec((1, n)) for n in sums],
        out_shape=[jax.ShapeDtypeStruct(shape, kind) for shape, kind in shapes],
        input_output_aliases=aliases,
        compiler_params=pltpu.CompilerParams(vmem_limit_bytes=60 * MIB),
        cost_estimate=lasting(66),
    )(*operands, *shared, *after)


def grad_rows(now, proj, cols, head, short, out, d_short, d_bias):
    tile, block = now.shape
    at_row = lax.broadcasted_iota(jnp.int32, (tile, block), 0)
    one = jnp.where(at_row == tile - 1, head[0:1, cols], pltpu.roll(now, tile - 1, 0))
    two = jnp.where(
        at_row == tile - 1,
        head[1:2, cols],
        jnp.where(at_row == tile - 2, head[0:1, cols], pltpu.roll(now, tile - 2, 0)),
    )
    head[:, cols] = now[:8]
    proj = proj.astype(f32)
    d_short[0:1, cols] += column_sum(two * proj)
    d_short[1:2, cols] += column_sum(one * proj)
    d_short[2:3, cols] += column_sum(now * proj)
    d_short[3:4, cols] += column_sum(now)
    grad = short[2:3, cols] * now + short[1:2, cols] * one + short[0:1, cols] * two
    grad = grad.astype(bf16)
    out[:, cols] = grad
    d_bias[:, cols] += column_sum(grad.astype(f32))


def gate_kernel(tiles, ggo_ref, proj_ref, rim_ref, short, *refs):
    out, d_short, d_bias, token, head = refs[-5:]
    i = pl.program_id(0)
    dim = ggo_ref.shape[1]
    token[...] = jnp.zeros_like(token)

    @pl.when(i == 0)
    def _():
        d_short[...] = jnp.zeros_like(d_short)
        d_bias[...] = jnp.zeros_like(d_bias)

    @pl.when(i % tiles == 0)
    def _():
        head[...] = rim_ref[...]

    block = 256
    for first in range(0, dim, block):
        cols = slice(first, first + block)
        grad_rows(ggo_ref[:, cols].astype(f32), proj_ref[:, cols], cols, head, short, out, d_short,
                  d_bias)


def gate_grads(seqs, ggo, proj, rims, short, after):
    tok, dim = ggo.shape
    width = tok // seqs
    tile = min(256, width)
    tiles = width // tile
    by_row = pl.BlockSpec(
        (tile, dim), lambda i: ((i // tiles) * tiles + tiles - 1 - i % tiles, 0)
    )
    return pl.pallas_call(
        functools.partial(gate_kernel, tiles),
        grid=(seqs * tiles,),
        in_specs=[
            by_row,
            by_row,
            pl.BlockSpec((None, 8, dim), lambda i: (i // tiles, 0, 0)),
            once((4, dim)),
        ]
        + [ANYWHERE] * len(after),
        out_specs=[by_row, whole_spec((4, dim)), whole_spec((1, dim)), whole_spec(TOKEN.shape)],
        out_shape=[
            jax.ShapeDtypeStruct((tok, dim), bf16),
            jax.ShapeDtypeStruct((4, dim), f32),
            jax.ShapeDtypeStruct((1, dim), f32),
            TOKEN,
        ],
        scratch_shapes=[pltpu.VMEM((8, dim), f32)],
        compiler_params=pltpu.CompilerParams(vmem_limit_bytes=60 * MIB),
        cost_estimate=lasting(7),
    )(ggo, proj, rims, short, *after)


def pair_kernel(gback_ref, gconv_ref, gates_ref, proj_ref, rim_ref, skip, short, *refs):
    out, d_short, d_bias, token, head = refs[-5:]
    i = pl.program_id(0)
    wide = rim_ref.shape[1]
    dim = wide // 2
    token[...] = jnp.zeros_like(token)

    @pl.when(i == 0)
    def _():
        head[...] = rim_ref[...]
        d_short[...] = jnp.zeros_like(d_short)
        d_bias[...] = jnp.zeros_like(d_bias)

    grad_carried = joined(gback_ref).astype(f32) + skip[...] * joined(gconv_ref).astype(f32)
    block = 256
    for first in range(0, dim, block):
        grad = grad_carried[:, first : first + block]
        for stream in range(2):
            cols = slice(stream * dim + first, stream * dim + first + block)
            other = slice(dim + (1 - stream) * dim + first, dim + (1 - stream) * dim + first + block)
            past = slice(dim + cols.start, dim + cols.stop)
            now = grad * gates_ref[:, other].astype(f32)
            grad_rows(now, proj_ref[:, past], cols, head, short, out, d_short, d_bias)


def pair_grads(s, seqs, gback, gconv, mixed, proj, rim, skip, short, shared, after):
    blocks, width, chans = gback.shape
    wide3 = mixed.shape[1]
    dim = blocks * chans
    wide = 2 * dim
    tile = min(256, width)
    tiles = width // tile
    back_row = lambda cols: pl.BlockSpec((tile, cols), lambda i: (s * tiles + tiles - 1 - i, 0))
    split = pl.BlockSpec((blocks, tile, chans), lambda i: (0, tiles - 1 - i, 0))
    operands = (gback, gconv, mixed, proj, rim, skip, short)
    return pl.pallas_call(
        pair_kernel,
        grid=(tiles,),
        in_specs=[
            split,
            split,
            back_row(wide3),
            back_row(wide3),
            once((8, wide)),
            once((1, dim)),
            once((4, wide)),
        ]
        + [ANYWHERE] * (len(shared) + len(after)),
        out_specs=[
            back_row(wide),
            whole_spec((4, wide)),
            whole_spec((1, wide)),
            whole_spec(TOKEN.shape),
        ],
        out_shape=[
            jax.ShapeDtypeStruct((seqs * width, wide), bf16),
            jax.ShapeDtypeStruct((4, wide), f32),
            jax.ShapeDtypeStruct((1, wide), f32),
            TOKEN,
        ],
        input_output_aliases={len(operands) + n: n for n in range(len(shared))},
        scratch_shapes=[pltpu.VMEM((8, wide), f32)],
        compiler_params=pltpu.CompilerParams(vmem_limit_bytes=60 * MIB),
        cost_estimate=lasting(11),
    )(*operands, *shared, *after)


def input_kernel(first_ref, rest_ref, x_ref, resid_ref, gain, w_ref, *refs):
    igrad_ref, d_gain, d_shift, token = refs[-4:]
    dim = x_ref.shape[1]
    token[...] = jnp.zeros_like(token)

    @pl.when(pl.program_id(0) == 0)
    def _():
        d_gain[...] = jnp.zeros_like(d_gain)
        d_shift[...] = jnp.zeros_like(d_shift)

    grad = dot_t(first_ref[...], w_ref[:, :dim]) + dot_t(rest_ref[...], w_ref[:, dim:])
    xhat, root = normalized(x_ref[...].astype(f32))
    d_shift[...] += column_sum(grad)
    d_gain[...] += column_sum(grad * xhat)
    igrad_ref[...] = resid_ref[...] + norm_back(grad, gain[...], xhat, root)


def input_grads(s, first, rest, inputs, resid, gain, weight, shared, after):
    seqs, width, dim = inputs.shape
    wide = weight.shape[1]
    tile = min(256, width)
    tiles = width // tile
    stacked = lambda cols: pl.BlockSpec((tile, cols), lambda i: (s * tiles + i, 0))
    layer = pl.BlockSpec((None, tile, dim), lambda i: (s, i, 0))
    operands = (first, rest, inputs, resid, gain, weight)
    return pl.pallas_call(
        input_kernel,
        grid=(tiles,),
        in_specs=[
            stacked(dim),
            stacked(wide - dim),
            layer,
            stacked(dim),
            once((1, dim)),
            once((dim, wide)),
        ]
        + [ANYWHERE] * (len(shared) + len(after)),
        out_specs=[layer, whole_spec((1, dim)), whole_spec((1, dim)), whole_spec(TOKEN.shape)],
        out_shape=[
            jax.ShapeDtypeStruct((seqs, width, dim), f32),
            jax.ShapeDtypeStruct((1, dim), f32),
            jax.ShapeDtypeStruct((1, dim), f32),
            TOKEN,
        ],
        input_output_aliases={len(operands) + n: n for n in range(len(shared))},
        compiler_params=pltpu.CompilerParams(vmem_limit_bytes=60 * MIB),
        cost_estimate=lasting(14),
    )(*operands, *shared, *after)


def over_tokens(left, right):
    return lax.dot_general(left, right, (((0,), (0,)), ((), ())), preferred_element_type=f32)


def tall_kernel(left, right, *refs):
    out, token = refs[-2:]
    token[...] = jnp.zeros_like(token)
    total = over_tokens(left[...], right[...])
    rows = out.shape[3]
    for b in range(out.shape[1]):
        out[0, b, 0] = total[b * rows : (b + 1) * rows].astype(bf16)


def flat_kernel(left, right, *refs):
    out, token = refs[-2:]
    token[...] = jnp.zeros_like(token)
    total = over_tokens(left[...], right[...])
    cores, buckets, zs, rows, _ = out.shape
    for z in range(zs):
        for c in range(cores):
            for b in range(buckets):
                at = ((cores * z + c) * buckets + b) * rows
                out[c, b, z] = total[at : at + rows].astype(bf16)


def two_kernel(steps, left, right, left2, right2, *refs):
    i = pl.program_id(0)

    @pl.when(i < steps)
    def _():
        flat_kernel(left, right, *refs)

    @pl.when(i >= steps)
    def _():
        flat_kernel(left2, right2, *refs)


def two_weight_grads(left, right, left2, right2, parts, buckets, after):
    tok, high = left.shape
    cols = right.shape[1]
    rows = high // parts // buckets
    if rows % 32:
        one, _ = weight_grad(left, right, parts, buckets, after)
        two, _ = weight_grad(left2, right2, parts, buckets, after)
        return jnp.concatenate([one, two], axis=1), after[0]
    block = min(512, cols)
    steps = cols // block
    shape = (2, buckets, parts // 2, rows, 2 * cols)
    total, token = pl.pallas_call(
        functools.partial(two_kernel, steps),
        grid=(2 * steps,),
        in_specs=[
            once((tok, high)),
            pl.BlockSpec((tok, block), lambda i: (0, jnp.minimum(i, steps - 1))),
            once((tok, high)),
            pl.BlockSpec((tok, block), lambda i: (0, jnp.maximum(i - steps, 0))),
        ]
        + [ANYWHERE] * len(after),
        out_specs=[
            pl.BlockSpec(shape[:4] + (block,), lambda i: (0, 0, 0, 0, i)),
            whole_spec(TOKEN.shape),
        ],
        out_shape=[jax.ShapeDtypeStruct(shape, bf16), TOKEN],
        compiler_params=pltpu.CompilerParams(vmem_limit_bytes=60 * MIB),
        cost_estimate=lasting(18),
    )(left, right, left2, right2, *after)
    return total.reshape(high, 2 * cols), token


def weight_grad(left, right, parts, buckets, after):
    tok, high = left.shape
    cols = right.shape[1]
    share = high // parts
    rows = share // buckets
    shape = (2, buckets, parts // 2, rows, cols)
    if rows % 32:
        total = jnp.einsum("tk,tn->kn", left, right, preferred_element_type=f32).astype(bf16)
        total = total.reshape(parts // 2, 2, buckets, rows, cols)
        return jnp.transpose(total, (1, 2, 0, 3, 4)).reshape(high, cols), after[0]
    tall = share % 512 == 0
    block = min(512, cols)
    if tall:
        steps = parts
        specs = [pl.BlockSpec((tok, share), lambda i: (0, i)), once((tok, cols))]
        out = pl.BlockSpec((1, buckets, 1, rows, cols), lambda i: (i % 2, 0, i // 2, 0, 0))
    else:
        steps = cols // block
        specs = [once((tok, high)), pl.BlockSpec((tok, block), lambda i: (0, i))]
        out = pl.BlockSpec(shape[:4] + (block,), lambda i: (0, 0, 0, 0, i))
    total, token = pl.pallas_call(
        tall_kernel if tall else flat_kernel,
        grid=(steps,),
        in_specs=specs + [ANYWHERE] * len(after),
        out_specs=[out, whole_spec(TOKEN.shape)],
        out_shape=[jax.ShapeDtypeStruct(shape, bf16), TOKEN],
        compiler_params=pltpu.CompilerParams(vmem_limit_bytes=60 * MIB),
        cost_estimate=lasting(23),
    )(left, right, *after)
    return total.reshape(high, cols), token


def swapped(block, axis, groups=None):
    return lax.all_to_all(
        block, axis, split_axis=0, concat_axis=0, tiled=True, axis_index_groups=groups
    )


def added(block):
    total = block[0].astype(f32)
    for n in range(1, block.shape[0]):
        total = total + block[n].astype(f32)
    return total


def tied(block, token):
    return block + (token[0, 0] * 0.0).astype(block.dtype)


def launch_kernel(*refs):
    refs[-1][...] = jnp.zeros_like(refs[-1])


def launched(block, after):
    return pl.pallas_call(
        launch_kernel,
        in_specs=[ANYWHERE] * (1 + len(after)),
        out_specs=[ANYWHERE, pl.BlockSpec(memory_space=pltpu.VMEM)],
        out_shape=[jax.ShapeDtypeStruct(block.shape, block.dtype), TOKEN],
        input_output_aliases={0: 0},
        cost_estimate=lasting(1),
    )(block, *after)


def pair_groups(parts):
    return [[2 * z, 2 * z + 1] for z in range(parts // 2)]


def pair_sum(block, parts):
    return lax.psum_scatter(
        block, "seq", scatter_dimension=0, tiled=True, axis_index_groups=pair_groups(parts)
    )


def bucket_sum(block):
    return lax.psum_scatter(block, "bucket", scatter_dimension=0, tiled=True)


def line_groups(parts):
    return [[2 * z + c for z in range(parts // 2)] for c in range(2)]


def line_scatter(block, parts):
    return lax.psum_scatter(
        block, "seq", scatter_dimension=0, tiled=True, axis_index_groups=line_groups(parts)
    )


def pair_swap(block, parts):
    block = block.reshape(2, -1, block.shape[1])
    return added(swapped(block, "seq", pair_groups(parts))).astype(bf16)


def bucket_swap(block, buckets):
    block = block.reshape(buckets, -1, block.shape[1])
    return added(swapped(block, "bucket")).astype(bf16)


def line_sum(block, parts):
    block = block.reshape(parts // 2, -1, block.shape[1])
    return added(swapped(block, "seq", line_groups(parts))).astype(bf16)


def shared_out(block, buckets):
    cols = block.shape[1]
    block = swapped(jnp.broadcast_to(block, (buckets,) + block.shape), "bucket")
    return block.reshape(-1, cols).astype(f32)


def on_device(
    inputs,
    cotangent,
    lengths,
    norm_gains,
    norm_biases,
    in_weight,
    in_bias,
    short_conv,
    long_skip,
    filter_in,
    filter_mid,
    filter_vecs,
    filter_out,
    decay,
    out_weight,
    out_bias,
    up_weight,
    up_bias,
    down_weight,
    down_bias,
):
    seqs, width, dim = inputs.shape
    parts = lax.axis_size("seq")
    index = lax.axis_index("seq")
    chans = dim // parts
    fits = chans % LANES == 0
    blocks = parts if fits else 1
    row = lambda v: v.reshape(1, -1)
    gain1, gain2 = norm_gains[0:1], norm_gains[1:2]
    shift1, shift2 = norm_biases[0:1], norm_biases[1:2]
    skip = row(long_skip)
    tables = transform_tables()

    def to_channels(block):
        if not fits:
            block = jnp.swapaxes(block.reshape(width, parts, chans), 0, 1)
        got = lax.all_to_all(block, "seq", split_axis=0, concat_axis=0, tiled=True)
        got = got.reshape(LEN, chans)
        return got if fits else jnp.pad(got, ((0, 0), (0, LANES - chans)))

    def to_positions(block):
        block = block[:, :chans].reshape(parts, width, chans)
        got = lax.all_to_all(block, "seq", split_axis=0, concat_axis=0, tiled=True)
        return got if fits else jnp.swapaxes(got, 0, 1).reshape(1, width, dim)

    rims = passed_along(inputs[:, width - 2 :, :], "seq", 1)
    rims = jnp.pad(rims, ((0, 0), (14, 0), (0, 0)))
    flag = (index > 0).astype(f32).reshape(1, 1)
    counts = jnp.clip(lengths - index * width, 0, width)

    buckets = lax.axis_size("bucket")

    start = index * chans
    columns = lax.dynamic_slice_in_dim(filter_out, start, chans, 1)
    rates = lax.dynamic_slice_in_dim(decay, start, chans, 0)

    network = (
        positions_table(),
        jnp.pad(filter_in.T, ((0, 0), (0, ROWS_E - EMB))),
        filter_mid.T,
        filter_vecs.T,
        jnp.pad(columns, ((0, 0), (0, LANES - chans))) if not fits else columns,
        row(jnp.pad(rates, (0, LANES - chans)) if not fits else rates),
    )
    data, carried = [], []
    shared = after = ()
    for s in range(seqs):
        got = front(s, inputs, rims, flag, gain1, shift1, in_weight, row(in_bias), short_conv,
                    blocks, shared, after)
        shared, token = got[:3], got[4]
        carried.append(got[3])
        data.append(to_channels(got[3]))
        if s == 0:
            taps_spec = taps_transform(network, tables, (token,))
            after = (taps_spec,)
    normed, proj, mixed = shared

    specs, convs = [], []
    for s in range(seqs):
        conv, spec, token = long_conv(data[s], taps_spec, tables, None, (token,))
        specs.append(spec)
        convs.append(to_positions(conv))

    mid_sums, grad_convs, grads = [], [], []
    shared = ()
    for s in range(seqs):
        got = middle(
            s, counts[s : s + 1], convs[s], carried[s], mixed, inputs, cotangent, skip, gain2,
            shift2, out_weight, row(out_bias), up_weight, row(up_bias), down_weight,
            row(down_bias), shared, (token,),
        )
        shared, token = got[:9], got[10]
        mid_sums.append(got[10:])
        grad_convs.append(got[9])
        grads.append(to_channels(got[9]))
    output, act, grad_hidden, normed2, gated, grad_down_in, grad_branch, resid, grad_gate = shared

    corrs, gbacks = [], []
    back, corr, token = long_conv(grads[0], taps_spec, tables, specs[0], (token,))
    corrs.append(corr)
    up, token = weight_grad(normed2, grad_hidden, parts, buckets, (token,))
    down, token = weight_grad(act, grad_down_in, parts, buckets, (token,))
    up, token = launched(up, (token, grads[-1]))
    up = pair_sum(up, parts)
    down, token = launched(down, (token,))
    down = pair_sum(down, parts)
    gbacks.append(to_positions(back))

    gate_rims = tied(grad_gate.reshape(seqs, width, dim)[:, :2], token)
    gate_rims = passed_along(gate_rims, "seq", -1).astype(f32)
    gate_rims = jnp.pad(gate_rims, ((0, 0), (0, 6), (0, 0)))

    for s in range(1, seqs):
        back, corr, token = long_conv(grads[s], taps_spec, tables, specs[s], (token,))
        corrs.append(corr)
        gbacks.append(to_positions(back))
    up, token = launched(up, (token,))
    up = bucket_sum(up)
    grad_first, d_short1, d_bias1, token = gate_grads(
        seqs, grad_gate, proj, gate_rims, short_conv[:, :dim], (token,)
    )
    both, token = two_weight_grads(
        gated, grad_branch, normed, grad_first, parts, buckets, (token,)
    )
    both, token = launched(both, (token, gbacks[0]))
    both = pair_sum(both, parts)
    down, token = launched(down, (token,))
    down = bucket_sum(down)

    def first_rows(block):
        return jnp.swapaxes(block[:, :2], 0, 1).reshape(2, dim).astype(f32)

    d_fin, d_fmid, d_fvecs, d_cols, token = taps_back(corrs, tables, network, (token,))
    gbacks[-1], token = launched(gbacks[-1], (token,))
    d_fin, d_fvecs, d_cols = d_fin[:EMB], d_fvecs.T, d_cols[:, :chans]

    rim_rows = []
    for s in range(seqs):
        grad_carried = first_rows(gbacks[s]) + skip * first_rows(grad_convs[s])
        edge = mixed[s * width : s * width + 2].astype(f32)
        rim_rows.append(
            jnp.concatenate(
                [grad_carried * edge[:, 2 * dim :], grad_carried * edge[:, dim : 2 * dim]], axis=1
            )
        )
    rim = passed_along(jnp.stack(rim_rows), "seq", -1)
    rim = jnp.pad(rim, ((0, 0), (0, 6), (0, 0)))
    pair_sums = []
    shared = ()
    both, token = launched(both, (token,))
    both = bucket_swap(both, buckets)
    up, token = launched(up, (token,))
    up = line_scatter(up, parts)
    shared = ()
    pair_sums = []
    for s in range(seqs):
        got = pair_grads(s, seqs, gbacks[s], grad_convs[s], mixed, proj, rim[s], skip,
                         short_conv[:, dim:], shared, (token,))
        shared, token = got[:1], got[3]
        pair_sums.append(got[1:3])
    grad_rest = shared[0]
    rest, token = weight_grad(normed, grad_rest, parts, buckets, (token, both))
    rest_half = pair_swap(rest, parts)
    rest = bucket_swap(rest_half, buckets)
    end_sums = []
    shared = ()
    hold = (rest_half,)
    for s in range(seqs):
        got = input_grads(s, grad_first, grad_rest, inputs, resid, gain1, in_weight, shared,
                          (token,) + hold)
        shared, token = got[:1], got[3]
        hold = ()
        if s == 0:
            down, token = launched(down, (token,))
            down = line_scatter(down, parts)
        end_sums.append(got[1:3])
    pair = jnp.concatenate([up.reshape(-1, dim), down], axis=0)
    pair = lax.all_gather(pair, "bucket", axis=0, tiled=True).astype(f32)
    pair = pair.reshape(buckets, 2, -1, dim)
    d_up_weight = pair[:, 0].reshape(dim // parts, -1)
    d_down_weight = pair[:, 1].reshape(-1, dim)
    last = line_sum(jnp.concatenate([both, rest], axis=1), parts)
    last = shared_out(last, buckets)
    d_out_weight, d_in_weight = last[:, :dim], last[:, dim:]
    input_grad = shared[0]

    def summed(lists, n):
        total = lists[0][n]
        for other in lists[1:]:
            total = total + other[n]
        return total

    small = [
        jnp.concatenate([summed(end_sums, 0), summed(mid_sums, 0)], axis=0),
        jnp.concatenate([summed(end_sums, 1), summed(mid_sums, 1)], axis=0),
        jnp.concatenate([d_bias1, summed(pair_sums, 1)], axis=1),
        jnp.concatenate([d_short1, summed(pair_sums, 0)], axis=1),
        summed(mid_sums, 5),
        d_fin,
        d_fmid,
        d_fvecs,
        summed(mid_sums, 4),
        summed(mid_sums, 3),
        summed(mid_sums, 2),
    ]
    flat = jnp.concatenate(
        [
            jnp.swapaxes(piece.reshape(piece.shape[0], parts, -1), 0, 1).reshape(parts, -1)
            for piece in small
        ],
        axis=1,
    )
    flat = added(swapped(tied(flat, rest), "seq"))
    flat = jnp.concatenate([flat, d_cols.reshape(-1)])
    flat = added(swapped(jnp.broadcast_to(flat, (buckets,) + flat.shape), "bucket"))
    shares = []
    at = 0
    for shape in [piece.shape for piece in small] + [d_cols.shape]:
        share = shape[1] if len(shares) == len(small) else shape[1] // parts
        shares.append(flat[at : at + shape[0] * share].reshape(shape[0], share))
        at += shape[0] * share
    (d_gains, d_shifts, d_in_bias, d_short, d_skip, d_fin, d_fmid, d_fvecs, d_out_b, d_up_b,
     d_down_b, d_fout) = shares

    return (
        output,
        input_grad,
        d_gains,
        d_shifts,
        d_in_weight,
        d_in_bias.reshape(-1),
        d_short,
        d_skip.reshape(-1),
        d_fin,
        d_fmid,
        d_fvecs,
        d_fout,
        d_out_weight,
        d_out_b.reshape(-1),
        d_up_weight,
        d_up_b.reshape(-1),
        d_down_weight,
        d_down_b.reshape(-1),
    )


def solution(mesh):
    whole = P()
    in_specs = (P("bucket", "seq", None),) * 2 + (P("bucket"),) + (whole,) * 17
    rows, cols, flat = P("seq", None), P(None, "seq"), P("seq")
    out_specs = (
        P("bucket", "seq", None),
        P("bucket", "seq", None),
        cols,
        cols,
        rows,
        flat,
        cols,
        flat,
        cols,
        cols,
        cols,
        cols,
        rows,
        flat,
        rows,
        flat,
        rows,
        flat,
    )
    return jax.shard_map(
        on_device, mesh=mesh, in_specs=in_specs, out_specs=out_specs, check_vma=False
    )
```
